32 devices in a mesh: img: 2 (over x), wide: 16 (over z, y, core).
Axes of the slice: x: 2, y: 2, z: 4, core: 2. Of those that a mesh axis runs over, the one named last changes fastest.
Arguments:
- latent: bfloat16 [64, 256, 320], P('img', 'wide'), parts along dimension 0, may hold values from -45 to 45
- group_norm_gain: float32 [320], replicated, may hold values from 0.25 to 1.75
- group_norm_shift: float32 [320], replicated, may hold values from -1.5 to 1.5
- kernel_weight: bfloat16 [3, 3, 320, 320], replicated, may hold values from -0.109375 to 0.109375
- kernel_bias: float32 [320], replicated, may hold values from -0.8 to 0.8
Outputs:
- mixed: bfloat16 [64, 256, 320], P('img', 'wide'), parts along dimension 0
The draws below stay inside these ranges and needn't reach their ends.
There are 2 independent parts, one for each index of `img`. The reference program is written for one: setup_inputs(seed, part) draws one part's arguments, and reference() takes and returns one part's arrays. A program takes and returns all parts, laid end to end along the dimension named above; an argument that names none is the same for every part. Nothing has to cross between parts.
All inputs are finite; a program needn't handle non-finite values.
Results may differ from the reference program's by a relative error of at most 0.0085.
Values may be sent and summed in bfloat16 or wider, within the bound.
No kernel may reach another device: no remote copies, remote signals or barrier semaphores. Data moves between devices by JAX's collectives and lax.ppermute only.
A program may use at most 64 MiB of HBM per device.

```python
import jax
import jax.numpy as jnp
from jax import lax

CHANNEL_COUNT = 320
NORM_GROUPS = 32
TILE = 128
OVER = 32
DILATION_FACTOR = 8
WINDOW_ROWS = 32
STRIDE = 96
LATENT_COLUMNS = 256
TILES = 3


def draw_latent(key, part):
    key_base, key_phase, key_col, key_row = jax.random.split(key, 4)
    full_shape = (WINDOW_ROWS, LATENT_COLUMNS, CHANNEL_COUNT)
    base_draw = jnp.clip(jax.random.normal(key_base, full_shape, jnp.float32), -5.0, 5.0)
    phase_shift = jax.random.uniform(key_phase, (), jnp.float32, 0.0, 6.2831853)
    col_index = jnp.arange(LATENT_COLUMNS, dtype=jnp.float32)
    smooth = jnp.exp(1.1512925 * jnp.sin(col_index * (6.2831853 / (4.0 * STRIDE)) + phase_shift))
    rough_col = jnp.exp(jax.random.uniform(key_col, (LATENT_COLUMNS,), jnp.float32, -0.35, 0.35))
    rough_row = jnp.exp(jax.random.uniform(key_row, (WINDOW_ROWS,), jnp.float32, -0.69, 0.69))
    scaled = base_draw * (smooth * rough_col)[None, :, None] * rough_row[:, None, None]
    return scaled.astype(jnp.bfloat16)


def centred(stream_key, dims, scale, bound, kind=jnp.bfloat16):
    array = scale * jax.random.normal(stream_key, dims, jnp.float32)
    return jnp.clip(array, min=-bound, max=bound).astype(kind)


def setup_inputs(seed: int = 0, part: int = 0) -> dict:
    key_list = jax.random.split(jax.random.key(seed), 6)
    own_keys = jax.random.split(jax.random.fold_in(key_list[5], part), 6)
    return {
        "latent": draw_latent(jax.random.fold_in(jax.random.fold_in(key_list[5], part), 71), part),
        "group_norm_gain": jnp.clip(1.0 + 0.15 * jax.random.normal(key_list[1], (CHANNEL_COUNT,), jnp.float32), 0.25, 1.75),
        "group_norm_shift": centred(key_list[2], (CHANNEL_COUNT,), 0.3, 1.5, jnp.float32),
        "kernel_weight": centred(key_list[3], (3, 3, CHANNEL_COUNT, CHANNEL_COUNT), (9 * CHANNEL_COUNT) ** -0.5, 0.109375),
        "kernel_bias": centred(key_list[4], (CHANNEL_COUNT,), 0.2, 0.8, jnp.float32),
    }


epsilon = 1e-05

def apply_kernel(apply_silu, weight, offset, spacing):
    result = lax.conv_general_dilated(apply_silu.astype(jnp.float32)[None], weight.astype(jnp.float32), (1, 1), ((spacing, spacing), (spacing, spacing)), rhs_dilation=(spacing, spacing), dimension_numbers=('NHWC', 'HWIO', 'NHWC'), precision=lax.Precision.HIGHEST)
    return (result[0] + offset).astype(jnp.bfloat16)

def group_normalize(value_array, mean_value, inverse, group_norm_gain, group_norm_shift):
    return jax.nn.silu((value_array - mean_value) * inverse * group_norm_gain + group_norm_shift)

def reference(latent, group_norm_gain, group_norm_shift, kernel_weight, kernel_bias):
    half_over = OVER // 2
    channels_per_group = CHANNEL_COUNT // NORM_GROUPS
    padded_width = STRIDE * (TILES - 1) + TILE
    padded = jnp.pad(latent, ((0, 0), (half_over, padded_width - half_over - LATENT_COLUMNS), (0, 0)))
    ramp_pos = jnp.arange(TILE, dtype=jnp.float32)
    ramp = jnp.minimum(ramp_pos + 1.0, TILE - ramp_pos)

    def one_tile(tile_index, carry):
        numer, denom = carry
        start_col = (tile_index * STRIDE).astype(jnp.int32)
        window = lax.dynamic_slice_in_dim(padded, start_col, TILE, 1).astype(jnp.float32)
        columns = tile_index * STRIDE - half_over + jnp.arange(TILE, dtype=jnp.int32)
        inside = ((columns >= 0) & (columns < LATENT_COLUMNS)).astype(jnp.float32)
        window = window * inside[None, :, None]
        grouped = window.reshape(WINDOW_ROWS, TILE, NORM_GROUPS, channels_per_group)
        running = lax.optimization_barrier(jnp.sum(grouped, axis=(0, 1, 3)))
        squares = lax.optimization_barrier(jnp.sum(grouped * grouped, axis=(0, 1, 3)))
        entry_items = WINDOW_ROWS * channels_per_group * jnp.sum(inside)
        mean_group = running / entry_items
        inverse = lax.rsqrt(squares / entry_items - mean_group * mean_group + epsilon)
        channel_mean = jnp.repeat(mean_group, channels_per_group)
        channel_inverse_scale = jnp.repeat(inverse, channels_per_group)
        apply_silu = (group_normalize(window, channel_mean, channel_inverse_scale, group_norm_gain, group_norm_shift) * inside[None, :, None]).astype(jnp.bfloat16)
        tile_out = apply_kernel(apply_silu, kernel_weight, kernel_bias, 1).astype(jnp.float32)
        old_numer = lax.dynamic_slice_in_dim(numer, start_col, TILE, 1)
        numer = lax.dynamic_update_slice_in_dim(numer, old_numer + ramp[None, :, None] * tile_out, start_col, 1)
        old_denom = lax.dynamic_slice_in_dim(denom, start_col, TILE, 0)
        denom = lax.dynamic_update_slice_in_dim(denom, old_denom + ramp, start_col, 0)
        return (numer, denom)
    numer0 = jnp.zeros((WINDOW_ROWS, padded_width, CHANNEL_COUNT), jnp.float32)
    denom0 = jnp.zeros((padded_width,), jnp.float32)
    numer, denom = lax.fori_loop(0, TILES, one_tile, (numer0, denom0))
    local_path = numer[:, half_over:half_over + LATENT_COLUMNS] / denom[half_over:half_over + LATENT_COLUMNS][None, :, None]
    value_array = latent.astype(jnp.float32).reshape(WINDOW_ROWS // DILATION_FACTOR, DILATION_FACTOR, LATENT_COLUMNS // DILATION_FACTOR, DILATION_FACTOR, NORM_GROUPS, channels_per_group)
    running = lax.optimization_barrier(jnp.sum(value_array, axis=(0, 2, 5)))
    squares = lax.optimization_barrier(jnp.sum(value_array * value_array, axis=(0, 2, 5)))
    entry_items = WINDOW_ROWS // DILATION_FACTOR * (LATENT_COLUMNS // DILATION_FACTOR) * channels_per_group
    mean_group = running / entry_items
    inverse = lax.rsqrt(squares / entry_items - mean_group * mean_group + epsilon)
    channel_mean = jnp.repeat(mean_group, channels_per_group, axis=2)[None, :, None, :, :]
    channel_inverse_scale = jnp.repeat(inverse, channels_per_group, axis=2)[None, :, None, :, :]
    apply_silu = group_normalize(value_array.reshape(WINDOW_ROWS // DILATION_FACTOR, DILATION_FACTOR, LATENT_COLUMNS // DILATION_FACTOR, DILATION_FACTOR, CHANNEL_COUNT), channel_mean, channel_inverse_scale, group_norm_gain, group_norm_shift).astype(jnp.bfloat16).reshape(WINDOW_ROWS, LATENT_COLUMNS, CHANNEL_COUNT)
    dilated_branch = apply_kernel(apply_silu, kernel_weight, kernel_bias, DILATION_FACTOR)
    return (0.5 * (local_path + dilated_branch.astype(jnp.float32))).astype(jnp.bfloat16)
```

```python
import jax
import jax.numpy as jnp
from jax import lax
from jax.experimental import pallas as pl
from jax.experimental.pallas import tpu as pltpu
from jax.sharding import PartitionSpec as P

NORM_GROUPS = 32
TILE = 128
OVER = 32
DIL = 8
STRIDE = 96
EPS = 1e-05
F32 = jnp.float32
BF16 = jnp.bfloat16


def iota(shape, dim):
    return lax.broadcasted_iota(jnp.int32, shape, dim)


def group_onehot(channels, per_group, offset):
    lane = iota((128, channels), 0) - offset
    first = lane * per_group
    ch = iota((128, channels), 1)
    return ((ch >= first) & (ch < first + per_group) & (lane >= 0)).astype(F32)


def group_onehot_t(channels, per_group, offset):
    lane = iota((channels, 128), 1) - offset
    first = lane * per_group
    ch = iota((channels, 128), 0)
    return ((ch >= first) & (ch < first + per_group) & (lane >= 0)).astype(F32)


def make_stats(rows, cols, channels, tile_rows):
    per_group = channels // NORM_GROUPS
    rim_blocks = (OVER // 2) // cols
    stride_blocks = STRIDE // cols
    tile_blocks = TILE // cols

    def kernel(x_ref, stats_ref, ea_ref, eb_ref, s_ref, q_ref):
        block = lax.axis_index("wide")
        even = lax.rem(block, 2) == 0
        for a in range(0, DIL, 2):
            s = [jnp.zeros((8, channels), F32) for _ in range(2)]
            q = [jnp.zeros((8, channels), F32) for _ in range(2)]
            for rr in range(rows // DIL):
                pa, pb = [], []
                for u in range(2):
                    r = rr * DIL + a + u
                    x = x_ref[r * cols : (r + 1) * cols, :].astype(F32)
                    lo, hi = x[:8], x[8:]
                    s[u] += lo + hi
                    q[u] += lo * lo + hi * hi
                    pa.append(jnp.where(even, hi, lo))
                    pb.append(jnp.where(even, lo, hi))
                r0 = (rr * DIL + a) * 8
                ea_ref[r0 : r0 + 16, :] = jnp.concatenate(pa, axis=0).astype(BF16)
                eb_ref[r0 : r0 + 16, :] = jnp.concatenate(pb, axis=0).astype(BF16)
            for u in range(2):
                s_ref[(a + u) * 8 : (a + u) * 8 + 8, :] = s[u]
                q_ref[(a + u) * 8 : (a + u) * 8 + 8, :] = q[u]
        total = None
        for ref, half, offset in (
            (s_ref, 0, 0),
            (s_ref, 1, 32),
            (q_ref, 0, 64),
            (q_ref, 1, 96),
        ):
            term = jnp.dot(
                ref[half * 32 : half * 32 + 32, :],
                group_onehot_t(channels, per_group, offset),
                precision=lax.Precision.HIGHEST,
                preferred_element_type=F32,
            )
            total = term if total is None else total + term
        stats_ref[0:32, :] = total
        line = jnp.sum(total, axis=0, keepdims=True)
        line = jnp.broadcast_to(line, (8, 128))
        line = line + pltpu.roll(line, 96, 1)
        for k in range(tile_rows // 8):
            start = (iota((8, 128), 0) + 8 * k) * stride_blocks - rim_blocks
            covers = (block >= start) & (block < start + tile_blocks)
            stats_ref[32 + 8 * k : 40 + 8 * k, :] = jnp.where(covers, line, 0.0)

    return pl.pallas_call(
        kernel,
        out_shape=(
            jax.ShapeDtypeStruct((32 + tile_rows, 128), F32),
            jax.ShapeDtypeStruct((rows * 8, channels), BF16),
            jax.ShapeDtypeStruct((rows * 8, channels), BF16),
        ),
        scratch_shapes=[
            pltpu.VMEM((64, channels), F32),
            pltpu.VMEM((64, channels), F32),
        ],
        compiler_params=pltpu.CompilerParams(vmem_limit_bytes=16 * 2**20),
        name="block_stats",
    )


def make_main(rows, cols, channels, out_channels, tile_rows, count):
    per_group = channels // NORM_GROUPS
    rim = OVER // 2
    rim_blocks = rim // cols
    stride_blocks = STRIDE // cols
    tile_blocks = TILE // cols
    pixels = rows * cols
    main = (channels // 128) * 128
    rem = channels - main
    depth = 9 * channels
    sub_items = float((rows // DIL) * (cols // DIL) * count * per_group)
    all_rows = 32 + tile_rows

    def kernel(
        x_ref, ha_ref, hb_ref, stats_ref, gain_ref, shift_ref, bias_ref, w_hbm, o_ref,
        w_ref, a_ref, sub_ref, blend_ref, sc_ref, sh_ref, tsc_ref, tsh_ref, bw_ref, sem,
    ):
        copies = []
        for tap in range(9):
            i, j = tap // 3, tap % 3
            copies.append(
                pltpu.make_async_copy(
                    w_hbm.at[i, j, pl.ds(0, main), :],
                    w_ref.at[pl.ds(tap * main, main), :],
                    sem.at[2 * tap],
                )
            )
            copies.append(
                pltpu.make_async_copy(
                    w_hbm.at[i, j, pl.ds(main, rem), :],
                    w_ref.at[pl.ds(9 * main + tap * rem, rem), :],
                    sem.at[2 * tap + 1],
                )
            )
        for c in copies:
            c.start()

        block = lax.axis_index("wide")
        even = lax.rem(block, 2) == 0
        tile0 = lax.div(block + rim_blocks, stride_blocks)
        tile1 = tile0 - 1

        stats = stats_ref[...]
        row_id = iota((all_rows, 128), 0)
        lane_id = iota((all_rows, 128), 1)
        start = (row_id - 32) * stride_blocks - rim_blocks
        blocks = jnp.minimum(start + tile_blocks, count) - jnp.maximum(start, 0)
        tile_items = jnp.maximum(blocks, 1).astype(F32) * float(pixels * per_group)
        is_sub = row_id < 32
        items = jnp.where(is_sub, sub_items, tile_items)
        mean = stats / items
        square = pltpu.roll(stats, 64, 1) / items
        inverse = lax.rsqrt(square - mean * mean + EPS)
        valid = lane_id < jnp.where(is_sub, 64, 32)
        mean = jnp.where(valid, mean, 0.0)
        inverse = jnp.where(valid, inverse, 0.0)
        both = jnp.concatenate([mean, inverse], axis=0)
        gain = 0.5 * gain_ref[...]
        shift = 0.5 * shift_ref[...]
        for half in range(2):
            wide = jnp.dot(
                both,
                group_onehot(channels, per_group, 32 * half),
                precision=lax.Precision.HIGHEST,
                preferred_element_type=F32,
            )
            scale = wide[all_rows:] * gain
            offset = shift - wide[:all_rows] * scale
            sc_ref[32 * half : 32 * half + 32, :] = scale[:32]
            sh_ref[32 * half : 32 * half + 32, :] = offset[:32]
            if half == 0:
                tile_row = iota((tile_rows, channels), 0)
                for t, tid in enumerate((tile0, tile1)):
                    pick = tile_row == jnp.maximum(tid, 0)
                    for ref, values in ((tsc_ref, scale), (tsh_ref, offset)):
                        line = jnp.sum(
                            jnp.where(pick, values[32:], 0.0), axis=0, keepdims=True
                        )
                        ref[8 * t : 8 * t + 8, :] = jnp.broadcast_to(line, (8, channels))

        sub_id = iota((8, channels), 0)
        for k in range(3):
            if k < 2:
                col = sub_id + 8 * k
            else:
                col = jnp.where(sub_id < 4, sub_id + cols, sub_id - 8)
            col = col + block * cols
            in_image = (col >= 0) & (col < count * cols)
            for j in range(3):
                out_col = col - (j - 1)
                ramps = []
                for tid in (tile0, tile1):
                    q = out_col - (tid * STRIDE - rim)
                    ok = (q >= 0) & (q < TILE) & (tid >= 0)
                    ramp = jnp.minimum(q + 1, TILE - q).astype(F32)
                    ramps.append(jnp.where(ok, ramp, 0.0))
                whole = jnp.maximum(ramps[0] + ramps[1], 1.0)
                for t, tid in enumerate((tile0, tile1)):
                    q = col - (tid * STRIDE - rim)
                    ok = (q >= 0) & (q < TILE) & in_image
                    bw_ref[j, k, t] = jnp.where(ok, ramps[t] / whole, 0.0)

        left_ok = jnp.where(block > 0, 1.0, 0.0).astype(F32)
        right_ok = jnp.where(block < count - 1, 1.0, 0.0).astype(F32)

        for r in range(DIL):
            sub_ref[r] = jnp.zeros((4 * 8, channels), F32)
            sub_ref[rows + DIL + r] = jnp.zeros((4 * 8, channels), F32)
        for j in range(3):
            blend_ref[j, 0] = jnp.zeros((cols, channels), F32)
            blend_ref[j, rows + 1] = jnp.zeros((cols, channels), F32)

        def silu(x, scale, offset):
            h = x * scale + offset
            return h + h * jnp.tanh(h)

        def activate(m, carry):
            ha = ha_ref[pl.ds(pl.multiple_of(16 * m, 16), 16), :].astype(F32)
            hb = hb_ref[pl.ds(pl.multiple_of(16 * m, 16), 16), :].astype(F32)
            left = jnp.where(even, hb, ha)
            right = jnp.where(even, ha, hb)
            for u in range(2):
                r = 2 * m + u
                x = x_ref[pl.ds(pl.multiple_of(r * cols, cols), cols), :].astype(F32)
                xl, xr = left[8 * u : 8 * u + 8], right[8 * u : 8 * u + 8]
                x0, x1 = x[:8], x[8:]
                res = pl.multiple_of(lax.rem(r, DIL) * 8, 8)
                scale = sc_ref[pl.ds(res, 8), :]
                offset = sh_ref[pl.ds(res, 8), :]
                sub_ref[r + DIL, 0:8, :] = silu(xl, scale, offset) * left_ok
                sub_ref[r + DIL, 8:16, :] = silu(x0, scale, offset)
                sub_ref[r + DIL, 16:24, :] = silu(x1, scale, offset)
                sub_ref[r + DIL, 24:32, :] = silu(xr, scale, offset) * right_ok
                xh = jnp.where(sub_id < 4, xr, xl)
                acts = [
                    [silu(v, tsc_ref[8 * t : 8 * t + 8, :], tsh_ref[8 * t : 8 * t + 8, :]) for t in range(2)]
                    for v in (x0, x1, xh)
                ]

                def mix(j, k):
                    return bw_ref[j, k, 0] * acts[k][0] + bw_ref[j, k, 1] * acts[k][1]

                blend_ref[1, r + 1, 0:8, :] = mix(1, 0)
                blend_ref[1, r + 1, 8:16, :] = mix(1, 1)
                f = [pltpu.roll(mix(2, k), 7, 0) for k in range(3)]
                blend_ref[2, r + 1, 0:8, :] = jnp.where(sub_id < 7, f[0], f[1])
                blend_ref[2, r + 1, 8:16, :] = jnp.where(sub_id < 7, f[1], f[2])
                g = [pltpu.roll(mix(0, k), 1, 0) for k in range(3)]
                blend_ref[0, r + 1, 0:8, :] = jnp.where(sub_id > 0, g[0], g[2])
                blend_ref[0, r + 1, 8:16, :] = jnp.where(sub_id > 0, g[1], g[0])
            return carry

        lax.fori_loop(0, rows // 2, activate, 0)

        def gather(r, carry):
            at = pl.ds(pl.multiple_of(r * cols, cols), cols)
            held = None
            for tap in range(9):
                i, j = tap // 3, tap % 3
                v = (
                    blend_ref[j, r + i] + sub_ref[r + DIL * i, 8 * j : 8 * j + cols, :]
                ).astype(BF16)
                a_ref[at, tap * main : (tap + 1) * main] = v[:, :main]
                if rem:
                    base = 9 * main + tap * rem
                    if tap % 2 == 0 and tap < 8:
                        held = v[:, main:]
                    elif tap < 8:
                        a_ref[at, base - rem : base + rem] = jnp.concatenate(
                            [held, v[:, main:]], axis=1
                        )
                    else:
                        a_ref[at, base : base + rem] = v[:, main:]
            return carry

        lax.fori_loop(0, rows, gather, 0)
        for c in copies:
            c.wait()
        acc = jnp.dot(a_ref[...], w_ref[...], preferred_element_type=F32)
        o_ref[...] = (0.5 * acc + bias_ref[...]).astype(BF16)

    vmem = pl.BlockSpec(memory_space=pltpu.VMEM)
    return pl.pallas_call(
        kernel,
        in_specs=[vmem] * 7 + [pl.BlockSpec(memory_space=pl.ANY)],
        out_specs=vmem,
        out_shape=jax.ShapeDtypeStruct((pixels, out_channels), BF16),
        scratch_shapes=[
            pltpu.VMEM((depth, out_channels), BF16),
            pltpu.VMEM((pixels, depth), BF16),
            pltpu.VMEM((rows + 2 * DIL, 4 * 8, channels), F32),
            pltpu.VMEM((3, rows + 2, cols, channels), F32),
            pltpu.VMEM((64, channels), F32),
            pltpu.VMEM((64, channels), F32),
            pltpu.VMEM((16, channels), F32),
            pltpu.VMEM((16, channels), F32),
            pltpu.VMEM((3, 3, 2, 8, channels), F32),
            pltpu.SemaphoreType.DMA((18,)),
        ],
        compiler_params=pltpu.CompilerParams(vmem_limit_bytes=40 * 2**20),
        name="norm_conv",
    )


def make_local(count):
    def local(latent, gain, shift, weight, bias):
        rows, cols, channels = latent.shape
        out_channels = weight.shape[3]
        stride_blocks = STRIDE // cols
        tiles = -(-(count + (OVER // 2) // cols) // stride_blocks)
        tile_rows = -(-tiles // 8) * 8
        x = latent.reshape(rows * cols, channels)
        stats, edge_a, edge_b = make_stats(rows, cols, channels, tile_rows)(x)
        pairs_a = [(i, i ^ 1) for i in range(count)]
        pairs_b = []
        for i in range(1, count - 1, 2):
            pairs_b += [(i, i + 1), (i + 1, i)]
        halo_a = lax.ppermute(edge_a, "wide", pairs_a)
        halo_b = lax.ppermute(edge_b, "wide", pairs_b)
        step = 1
        while step < count:
            stats = stats + lax.ppermute(stats, "wide", [(i, i ^ step) for i in range(count)])
            step *= 2
        out = make_main(rows, cols, channels, out_channels, tile_rows, count)(
            x, halo_a, halo_b, stats, gain[None], shift[None], bias[None], weight
        )
        return out.reshape(rows, cols, out_channels)

    return local


def solution(mesh):
    in_specs = (P("img", "wide", None), P(), P(), P(), P())
    out_specs = P("img", "wide", None)
    return jax.shard_map(
        make_local(mesh.shape["wide"]),
        mesh=mesh,
        in_specs=in_specs,
        out_specs=out_specs,
        check_vma=False,
    )
```

```python
import jax
import jax.numpy as jnp
from jax import lax
from jax.experimental import pallas as pl
from jax.experimental.pallas import tpu as pltpu
from jax.sharding import PartitionSpec as P

NORM_GROUPS = 32
TILE = 128
OVER = 32
DIL = 8
STRIDE = 96
EPS = 1e-05
F32 = jnp.float32
BF16 = jnp.bfloat16


def iota(shape, dim):
    return lax.broadcasted_iota(jnp.int32, shape, dim)


def group_onehot(channels, per_group, offset):
    lane = iota((128, channels), 0) - offset
    first = lane * per_group
    ch = iota((128, channels), 1)
    return ((ch >= first) & (ch < first + per_group) & (lane >= 0)).astype(F32)


def group_onehot_t(channels, per_group, offset):
    lane = iota((channels, 128), 1) - offset
    first = lane * per_group
    ch = iota((channels, 128), 0)
    return ((ch >= first) & (ch < first + per_group) & (lane >= 0)).astype(F32)


def make_stats(rows, cols, channels, tile_rows):
    per_group = channels // NORM_GROUPS
    rim_blocks = (OVER // 2) // cols
    stride_blocks = STRIDE // cols
    tile_blocks = TILE // cols

    def kernel(x_ref, stats_ref, ea_ref, eb_ref, near_ref, s_ref, q_ref):
        block = lax.axis_index("wide")
        even = lax.rem(block, 2) == 0
        for a in range(0, DIL, 2):
            s = [jnp.zeros((8, channels), F32) for _ in range(2)]
            q = [jnp.zeros((8, channels), F32) for _ in range(2)]
            for rr in range(rows // DIL):
                pa, pb = [], []
                for u in range(2):
                    r = rr * DIL + a + u
                    x = x_ref[r * cols : (r + 1) * cols, :]
                    near_ref[r * cols : (r + 1) * cols, :] = x
                    x = x.astype(F32)
                    lo, hi = x[:8], x[8:]
                    s[u] += lo + hi
                    q[u] += lo * lo + hi * hi
                    pa.append(jnp.where(even, hi, lo))
                    pb.append(jnp.where(even, lo, hi))
                r0 = (rr * DIL + a) * 8
                ea_ref[r0 : r0 + 16, :] = jnp.concatenate(pa, axis=0).astype(BF16)
                eb_ref[r0 : r0 + 16, :] = jnp.concatenate(pb, axis=0).astype(BF16)
            for u in range(2):
                s_ref[(a + u) * 8 : (a + u) * 8 + 8, :] = s[u]
                q_ref[(a + u) * 8 : (a + u) * 8 + 8, :] = q[u]
        total = None
        for ref, half, offset in (
            (s_ref, 0, 0),
            (s_ref, 1, 32),
            (q_ref, 0, 64),
            (q_ref, 1, 96),
        ):
            term = jnp.dot(
                ref[half * 32 : half * 32 + 32, :],
                group_onehot_t(channels, per_group, offset),
                precision=lax.Precision.HIGHEST,
                preferred_element_type=F32,
            )
            total = term if total is None else total + term
        stats_ref[0:32, :] = total
        line = jnp.sum(total, axis=0, keepdims=True)
        line = jnp.broadcast_to(line, (8, 128))
        line = line + pltpu.roll(line, 96, 1)
        for k in range(tile_rows // 8):
            start = (iota((8, 128), 0) + 8 * k) * stride_blocks - rim_blocks
            covers = (block >= start) & (block < start + tile_blocks)
            stats_ref[32 + 8 * k : 40 + 8 * k, :] = jnp.where(covers, line, 0.0)

    return pl.pallas_call(
        kernel,
        out_shape=(
            jax.ShapeDtypeStruct((32 + tile_rows, 128), F32),
            jax.ShapeDtypeStruct((rows * 8, channels), BF16),
            jax.ShapeDtypeStruct((rows * 8, channels), BF16),
            jax.ShapeDtypeStruct((rows * cols, channels), BF16),
        ),
        scratch_shapes=[
            pltpu.VMEM((64, channels), F32),
            pltpu.VMEM((64, channels), F32),
        ],
        compiler_params=pltpu.CompilerParams(vmem_limit_bytes=16 * 2**20),
        name="block_stats",
    )


def make_main(rows, cols, channels, out_channels, tile_rows, count):
    per_group = channels // NORM_GROUPS
    rim = OVER // 2
    rim_blocks = rim // cols
    stride_blocks = STRIDE // cols
    tile_blocks = TILE // cols
    pixels = rows * cols
    main = (channels // 128) * 128
    rem = channels - main
    depth = 9 * channels
    sub_items = float((rows // DIL) * (cols // DIL) * count * per_group)
    all_rows = 32 + tile_rows

    def kernel(
        x_ref, ha_ref, hb_ref, stats_ref, vec_ref, w_hbm, o_ref,
        w_ref, bw_ref, sem, a_ref, sub_ref, blend_ref, sc_ref, sh_ref, tsc_ref, tsh_ref,
    ):
        copies = []
        for tap in range(9):
            i, j = tap // 3, tap % 3
            copies.append(
                pltpu.make_async_copy(
                    w_hbm.at[i, j, pl.ds(0, main), :],
                    w_ref.at[pl.ds(tap * main, main), :],
                    sem.at[2 * tap],
                )
            )
            copies.append(
                pltpu.make_async_copy(
                    w_hbm.at[i, j, pl.ds(main, rem), :],
                    w_ref.at[pl.ds(9 * main + tap * rem, rem), :],
                    sem.at[2 * tap + 1],
                )
            )
        for c in copies:
            c.start()

        block = lax.axis_index("wide")
        even = lax.rem(block, 2) == 0
        tile0 = lax.div(block + rim_blocks, stride_blocks)
        tile1 = tile0 - 1

        stats = stats_ref[...]
        row_id = iota((all_rows, 128), 0)
        lane_id = iota((all_rows, 128), 1)
        start = (row_id - 32) * stride_blocks - rim_blocks
        blocks = jnp.minimum(start + tile_blocks, count) - jnp.maximum(start, 0)
        tile_items = jnp.maximum(blocks, 1).astype(F32) * float(pixels * per_group)
        is_sub = row_id < 32
        items = jnp.where(is_sub, sub_items, tile_items)
        mean = stats / items
        square = pltpu.roll(stats, 64, 1) / items
        inverse = lax.rsqrt(square - mean * mean + EPS)
        valid = lane_id < jnp.where(is_sub, 64, 32)
        mean = jnp.where(valid, mean, 0.0)
        inverse = jnp.where(valid, inverse, 0.0)
        both = jnp.concatenate([mean, inverse], axis=0)
        gain = vec_ref[0:1, :]
        shift = vec_ref[1:2, :]
        for half in range(2):
            wide = jnp.dot(
                both,
                group_onehot(channels, per_group, 32 * half),
                precision=lax.Precision.HIGHEST,
                preferred_element_type=F32,
            )
            scale = wide[all_rows:] * gain
            offset = shift - wide[:all_rows] * scale
            sc_ref[32 * half : 32 * half + 32, :] = scale[:32]
            sh_ref[32 * half : 32 * half + 32, :] = offset[:32]
            if half == 0:
                tile_row = iota((tile_rows, channels), 0)
                for t, tid in enumerate((tile0, tile1)):
                    pick = tile_row == jnp.maximum(tid, 0)
                    for ref, values in ((tsc_ref, scale), (tsh_ref, offset)):
                        line = jnp.sum(
                            jnp.where(pick, values[32:], 0.0), axis=0, keepdims=True
                        )
                        ref[8 * t : 8 * t + 8, :] = jnp.broadcast_to(line, (8, channels))

        left_ok = jnp.where(block > 0, 1.0, 0.0).astype(F32)
        right_ok = jnp.where(block < count - 1, 1.0, 0.0).astype(F32)

        for r in range(DIL):
            sub_ref[r] = jnp.zeros((4 * 8, channels), F32)
            sub_ref[rows + DIL + r] = jnp.zeros((4 * 8, channels), F32)
        for j in range(3):
            blend_ref[j, 0] = jnp.zeros((cols, channels), F32)
            blend_ref[j, rows + 1] = jnp.zeros((cols, channels), F32)

        sub_id = iota((8, channels), 0)
        for k in range(3):
            if k < 2:
                col = sub_id + 8 * k
            else:
                col = jnp.where(sub_id < 4, sub_id + cols, sub_id - 8)
            col = col + block * cols
            in_image = (col >= 0) & (col < count * cols)
            for j in range(3):
                out_col = col - (j - 1)
                ramps = []
                for tid in (tile0, tile1):
                    q = out_col - (tid * STRIDE - rim)
                    ok = (q >= 0) & (q < TILE) & (tid >= 0)
                    ramp = jnp.minimum(q + 1, TILE - q).astype(F32)
                    ramps.append(jnp.where(ok, ramp, 0.0))
                whole = jnp.maximum(ramps[0] + ramps[1], 1.0)
                for t, tid in enumerate((tile0, tile1)):
                    q = col - (tid * STRIDE - rim)
                    ok = (q >= 0) & (q < TILE) & in_image
                    bw_ref[j, k, t] = jnp.where(ok, ramps[t] / whole, 0.0)

        def silu(x, scale, offset):
            h = x * scale + offset
            return h + h * jnp.tanh(h)

        def activate(m, carry):
            ha = ha_ref[pl.ds(pl.multiple_of(16 * m, 16), 16), :].astype(F32)
            hb = hb_ref[pl.ds(pl.multiple_of(16 * m, 16), 16), :].astype(F32)
            left = jnp.where(even, hb, ha)
            right = jnp.where(even, ha, hb)
            for u in range(2):
                r = 2 * m + u
                x = x_ref[pl.ds(pl.multiple_of(r * cols, cols), cols), :].astype(F32)
                xl, xr = left[8 * u : 8 * u + 8], right[8 * u : 8 * u + 8]
                x0, x1 = x[:8], x[8:]
                res = pl.multiple_of(lax.rem(r, DIL) * 8, 8)
                scale = sc_ref[pl.ds(res, 8), :]
                offset = sh_ref[pl.ds(res, 8), :]
                sub_ref[r + DIL, 0:8, :] = silu(xl, scale, offset) * left_ok
                sub_ref[r + DIL, 8:16, :] = silu(x0, scale, offset)
                sub_ref[r + DIL, 16:24, :] = silu(x1, scale, offset)
                sub_ref[r + DIL, 24:32, :] = silu(xr, scale, offset) * right_ok
                xh = jnp.where(sub_id < 4, xr, xl)
                acts = [
                    [silu(v, tsc_ref[8 * t : 8 * t + 8, :], tsh_ref[8 * t : 8 * t + 8, :]) for t in range(2)]
                    for v in (x0, x1, xh)
                ]

                def mix(j, k):
                    return bw_ref[j, k, 0] * acts[k][0] + bw_ref[j, k, 1] * acts[k][1]

                blend_ref[1, r + 1, 0:8, :] = mix(1, 0)
                blend_ref[1, r + 1, 8:16, :] = mix(1, 1)
                f = [pltpu.roll(mix(2, k), 7, 0) for k in range(3)]
                blend_ref[2, r + 1, 0:8, :] = jnp.where(sub_id < 7, f[0], f[1])
                blend_ref[2, r + 1, 8:16, :] = jnp.where(sub_id < 7, f[1], f[2])
                g = [pltpu.roll(mix(0, k), 1, 0) for k in range(3)]
                blend_ref[0, r + 1, 0:8, :] = jnp.where(sub_id > 0, g[0], g[2])
                blend_ref[0, r + 1, 8:16, :] = jnp.where(sub_id > 0, g[1], g[0])
            return carry

        lax.fori_loop(0, rows // 2, activate, 0)

        def gather(r, carry):
            at = pl.ds(pl.multiple_of(r * cols, cols), cols)
            held = None
            for tap in range(9):
                i, j = tap // 3, tap % 3
                v = (
                    blend_ref[j, r + i] + sub_ref[r + DIL * i, 8 * j : 8 * j + cols, :]
                ).astype(BF16)
                a_ref[at, tap * main : (tap + 1) * main] = v[:, :main]
                if rem:
                    base = 9 * main + tap * rem
                    if tap % 2 == 0 and tap < 8:
                        held = v[:, main:]
                    elif tap < 8:
                        a_ref[at, base - rem : base + rem] = jnp.concatenate(
                            [held, v[:, main:]], axis=1
                        )
                    else:
                        a_ref[at, base : base + rem] = v[:, main:]
            return carry

        lax.fori_loop(0, rows, gather, 0, unroll=8)
        for c in copies:
            c.wait()
        acc = jnp.dot(a_ref[...], w_ref[...], preferred_element_type=F32)
        o_ref[...] = (0.5 * acc + vec_ref[2:3, :]).astype(BF16)

    vmem = pl.BlockSpec(memory_space=pltpu.VMEM)
    return pl.pallas_call(
        kernel,
        in_specs=[vmem] * 5 + [pl.BlockSpec(memory_space=pltpu.HBM)],
        out_specs=vmem,
        out_shape=jax.ShapeDtypeStruct((pixels, out_channels), BF16),
        scratch_shapes=[
            pltpu.VMEM((depth, out_channels), BF16),
            pltpu.VMEM((3, 3, 2, 8, channels), F32),
            pltpu.SemaphoreType.DMA((18,)),
            pltpu.VMEM((pixels, depth), BF16),
            pltpu.VMEM((rows + 2 * DIL, 4 * 8, channels), F32),
            pltpu.VMEM((3, rows + 2, cols, channels), F32),
            pltpu.VMEM((64, channels), F32),
            pltpu.VMEM((64, channels), F32),
            pltpu.VMEM((16, channels), F32),
            pltpu.VMEM((16, channels), F32),
        ],
        compiler_params=pltpu.CompilerParams(vmem_limit_bytes=52 * 2**20),
        name="norm_conv",
    )


def make_local(count):
    def local(latent, gain, shift, weight, bias):
        rows, cols, channels = latent.shape
        out_channels = weight.shape[3]
        stride_blocks = STRIDE // cols
        tiles = -(-(count + (OVER // 2) // cols) // stride_blocks)
        tile_rows = -(-tiles // 8) * 8
        x = latent.reshape(rows * cols, channels)
        stats, edge_a, edge_b, x_near = make_stats(rows, cols, channels, tile_rows)(x)
        pairs_a = [(i, i ^ 1) for i in range(count)]
        pairs_b = []
        for i in range(1, count - 1, 2):
            pairs_b += [(i, i + 1), (i + 1, i)]
        halo_a = lax.ppermute(edge_a, "wide", pairs_a)

        def summed(stats, step):
            return stats + lax.ppermute(stats, "wide", [(i, i ^ step) for i in range(count)])

        vectors = jnp.stack([0.5 * gain, 0.5 * shift, bias])
        step = 1
        while step < count:
            stats = summed(stats, step)
            if step == 2:
                edge_b, stats = lax.optimization_barrier((edge_b, stats))
                halo_b = lax.ppermute(edge_b, "wide", pairs_b)
            step *= 2
        out = make_main(rows, cols, channels, out_channels, tile_rows, count)(
            x_near, halo_a, halo_b, stats, vectors, weight
        )
        return out.reshape(rows, cols, out_channels)

    return local


def solution(mesh):
    in_specs = (P("img", "wide", None), P(), P(), P(), P())
    out_specs = P("img", "wide", None)
    return jax.shard_map(
        make_local(mesh.shape["wide"]),
        mesh=mesh,
        in_specs=in_specs,
        out_specs=out_specs,
        check_vma=False,
    )
```

```python
import jax
import jax.numpy as jnp
from jax import lax
from jax.experimental import pallas as pl
from jax.experimental.pallas import tpu as pltpu
from jax.sharding import PartitionSpec as P

NORM_GROUPS = 32
TILE = 128
OVER = 32
DIL = 8
STRIDE = 96
EPS = 1e-05
F32 = jnp.float32
BF16 = jnp.bfloat16


def iota(shape, dim):
    return lax.broadcasted_iota(jnp.int32, shape, dim)


def group_onehot(channels, per_group, offset):
    lane = iota((128, channels), 0) - offset
    first = lane * per_group
    ch = iota((128, channels), 1)
    return ((ch >= first) & (ch < first + per_group) & (lane >= 0)).astype(F32)


def group_onehot_t(channels, per_group, offset):
    lane = iota((channels, 128), 1) - offset
    first = lane * per_group
    ch = iota((channels, 128), 0)
    return ((ch >= first) & (ch < first + per_group) & (lane >= 0)).astype(F32)


def make_stats(rows, cols, channels, tile_rows):
    per_group = channels // NORM_GROUPS
    rim_blocks = (OVER // 2) // cols
    stride_blocks = STRIDE // cols
    tile_blocks = TILE // cols

    def kernel(x_ref, stats_ref, ea_ref, eb_ref, near_ref, s_ref, q_ref):
        block = lax.axis_index("wide")
        even = lax.rem(block, 2) == 0
        for a in range(0, DIL, 2):
            s = [jnp.zeros((8, channels), F32) for _ in range(2)]
            q = [jnp.zeros((8, channels), F32) for _ in range(2)]
            for rr in range(rows // DIL):
                pa, pb = [], []
                for u in range(2):
                    r = rr * DIL + a + u
                    x = x_ref[r * cols : (r + 1) * cols, :]
                    near_ref[r * cols : (r + 1) * cols, :] = x
                    x = x.astype(F32)
                    lo, hi = x[:8], x[8:]
                    s[u] += lo + hi
                    q[u] += lo * lo + hi * hi
                    pa.append(jnp.where(even, hi, lo))
                    pb.append(jnp.where(even, lo, hi))
                r0 = (rr * DIL + a) * 8
                ea_ref[r0 : r0 + 16, :] = jnp.concatenate(pa, axis=0).astype(BF16)
                eb_ref[r0 : r0 + 16, :] = jnp.concatenate(pb, axis=0).astype(BF16)
            for u in range(2):
                s_ref[(a + u) * 8 : (a + u) * 8 + 8, :] = s[u]
                q_ref[(a + u) * 8 : (a + u) * 8 + 8, :] = q[u]
        total = None
        for ref, half, offset in (
            (s_ref, 0, 0),
            (s_ref, 1, 32),
            (q_ref, 0, 64),
            (q_ref, 1, 96),
        ):
            term = jnp.dot(
                ref[half * 32 : half * 32 + 32, :],
                group_onehot_t(channels, per_group, offset),
                precision=lax.Precision.HIGHEST,
                preferred_element_type=F32,
            )
            total = term if total is None else total + term
        stats_ref[0:32, :] = total
        line = jnp.sum(total, axis=0, keepdims=True)
        line = jnp.broadcast_to(line, (8, 128))
        line = line + pltpu.roll(line, 96, 1)
        for k in range(tile_rows // 8):
            start = (iota((8, 128), 0) + 8 * k) * stride_blocks - rim_blocks
            covers = (block >= start) & (block < start + tile_blocks)
            stats_ref[32 + 8 * k : 40 + 8 * k, :] = jnp.where(covers, line, 0.0)

    return pl.pallas_call(
        kernel,
        out_shape=(
            jax.ShapeDtypeStruct((32 + tile_rows, 128), F32),
            jax.ShapeDtypeStruct((rows * 8, channels), BF16),
            jax.ShapeDtypeStruct((rows * 8, channels), BF16),
            jax.ShapeDtypeStruct((rows * cols, channels), BF16),
        ),
        scratch_shapes=[
            pltpu.VMEM((64, channels), F32),
            pltpu.VMEM((64, channels), F32),
        ],
        compiler_params=pltpu.CompilerParams(vmem_limit_bytes=16 * 2**20),
        name="block_stats",
    )


def make_blend(cols, channels, count):
    rim = OVER // 2

    def kernel(after_ref, bw_ref):
        block = lax.axis_index("wide")
        tile0 = lax.div(block + rim // cols, STRIDE // cols)
        tile1 = tile0 - 1
        sub_id = iota((8, channels), 0)
        for k in range(3):
            if k < 2:
                col = sub_id + 8 * k
            else:
                col = jnp.where(sub_id < 4, sub_id + cols, sub_id - 8)
            col = col + block * cols
            in_image = (col >= 0) & (col < count * cols)
            for j in range(3):
                out_col = col - (j - 1)
                ramps = []
                for tid in (tile0, tile1):
                    q = out_col - (tid * STRIDE - rim)
                    ok = (q >= 0) & (q < TILE) & (tid >= 0)
                    ramp = jnp.minimum(q + 1, TILE - q).astype(F32)
                    ramps.append(jnp.where(ok, ramp, 0.0))
                whole = jnp.maximum(ramps[0] + ramps[1], 1.0)
                for t, tid in enumerate((tile0, tile1)):
                    q = col - (tid * STRIDE - rim)
                    ok = (q >= 0) & (q < TILE) & in_image
                    bw_ref[j, k, t] = jnp.where(ok, ramps[t] / whole, 0.0)


    return pl.pallas_call(
        kernel,
        in_specs=[pl.BlockSpec(memory_space=pl.ANY)],
        out_specs=pl.BlockSpec(memory_space=pltpu.VMEM),
        out_shape=jax.ShapeDtypeStruct((3, 3, 2, 8, channels), F32),
        compiler_params=pltpu.CompilerParams(vmem_limit_bytes=16 * 2**20),
        cost_estimate=pl.CostEstimate(flops=5000000000, bytes_accessed=0, transcendentals=0),
        name="blend_weights",
    )


def make_main(rows, cols, channels, out_channels, tile_rows, count):
    per_group = channels // NORM_GROUPS
    rim = OVER // 2
    rim_blocks = rim // cols
    stride_blocks = STRIDE // cols
    tile_blocks = TILE // cols
    pixels = rows * cols
    main = (channels // 128) * 128
    rem = channels - main
    depth = 9 * channels
    sub_items = float((rows // DIL) * (cols // DIL) * count * per_group)
    all_rows = 32 + tile_rows

    def kernel(
        x_ref, ha_ref, hb_ref, stats_ref, vec_ref, bw_ref, w_hbm, o_ref,
        w_ref, sem, a_ref, sub_ref, blend_ref, sc_ref, sh_ref, tsc_ref, tsh_ref,
    ):
        copies = []
        for tap in range(9):
            i, j = tap // 3, tap % 3
            copies.append(
                pltpu.make_async_copy(
                    w_hbm.at[i, j, pl.ds(0, main), :],
                    w_ref.at[pl.ds(tap * main, main), :],
                    sem.at[2 * tap],
                )
            )
            copies.append(
                pltpu.make_async_copy(
                    w_hbm.at[i, j, pl.ds(main, rem), :],
                    w_ref.at[pl.ds(9 * main + tap * rem, rem), :],
                    sem.at[2 * tap + 1],
                )
            )
        for c in copies:
            c.start()

        block = lax.axis_index("wide")
        even = lax.rem(block, 2) == 0
        tile0 = lax.div(block + rim_blocks, stride_blocks)
        tile1 = tile0 - 1

        stats = stats_ref[...]
        row_id = iota((all_rows, 128), 0)
        lane_id = iota((all_rows, 128), 1)
        start = (row_id - 32) * stride_blocks - rim_blocks
        blocks = jnp.minimum(start + tile_blocks, count) - jnp.maximum(start, 0)
        tile_items = jnp.maximum(blocks, 1).astype(F32) * float(pixels * per_group)
        is_sub = row_id < 32
        items = jnp.where(is_sub, sub_items, tile_items)
        mean = stats / items
        square = pltpu.roll(stats, 64, 1) / items
        inverse = lax.rsqrt(square - mean * mean + EPS)
        valid = lane_id < jnp.where(is_sub, 64, 32)
        mean = jnp.where(valid, mean, 0.0)
        inverse = jnp.where(valid, inverse, 0.0)
        both = jnp.concatenate([mean, inverse], axis=0)
        vec = vec_ref[...].reshape(1, -1)
        wide_c = vec.shape[1] // 3
        gain = 0.5 * vec[:, :channels]
        shift = 0.5 * vec[:, wide_c : wide_c + channels]
        bias = vec[:, 2 * wide_c : 2 * wide_c + channels]
        for half in range(2):
            wide = jnp.dot(
                both,
                group_onehot(channels, per_group, 32 * half),
                precision=lax.Precision.HIGHEST,
                preferred_element_type=F32,
            )
            scale = wide[all_rows:] * gain
            offset = shift - wide[:all_rows] * scale
            sc_ref[32 * half : 32 * half + 32, :] = scale[:32]
            sh_ref[32 * half : 32 * half + 32, :] = offset[:32]
            if half == 0:
                tile_row = iota((tile_rows, channels), 0)
                for t, tid in enumerate((tile0, tile1)):
                    pick = tile_row == jnp.maximum(tid, 0)
                    for ref, values in ((tsc_ref, scale), (tsh_ref, offset)):
                        line = jnp.sum(
                            jnp.where(pick, values[32:], 0.0), axis=0, keepdims=True
                        )
                        ref[8 * t : 8 * t + 8, :] = jnp.broadcast_to(line, (8, channels))

        left_ok = jnp.where(block > 0, 1.0, 0.0).astype(F32)
        right_ok = jnp.where(block < count - 1, 1.0, 0.0).astype(F32)

        for r in range(DIL):
            sub_ref[r] = jnp.zeros((4 * 8, channels), F32)
            sub_ref[rows + DIL + r] = jnp.zeros((4 * 8, channels), F32)
        for j in range(3):
            blend_ref[j, 0] = jnp.zeros((cols, channels), F32)
            blend_ref[j, rows + 1] = jnp.zeros((cols, channels), F32)

        sub_id = iota((8, channels), 0)
        def silu(x, scale, offset):
            h = x * scale + offset
            return h + h * jnp.tanh(h)

        def activate(m, carry):
            ha = ha_ref[pl.ds(pl.multiple_of(16 * m, 16), 16), :].astype(F32)
            hb = hb_ref[pl.ds(pl.multiple_of(16 * m, 16), 16), :].astype(F32)
            left = jnp.where(even, hb, ha)
            right = jnp.where(even, ha, hb)
            for u in range(2):
                r = 2 * m + u
                x = x_ref[pl.ds(pl.multiple_of(r * cols, cols), cols), :].astype(F32)
                xl, xr = left[8 * u : 8 * u + 8], right[8 * u : 8 * u + 8]
                x0, x1 = x[:8], x[8:]
                res = pl.multiple_of(lax.rem(r, DIL) * 8, 8)
                scale = sc_ref[pl.ds(res, 8), :]
                offset = sh_ref[pl.ds(res, 8), :]
                sub_ref[r + DIL, 0:8, :] = silu(xl, scale, offset) * left_ok
                sub_ref[r + DIL, 8:16, :] = silu(x0, scale, offset)
                sub_ref[r + DIL, 16:24, :] = silu(x1, scale, offset)
                sub_ref[r + DIL, 24:32, :] = silu(xr, scale, offset) * right_ok
                xh = jnp.where(sub_id < 4, xr, xl)
                acts = [
                    [silu(v, tsc_ref[8 * t : 8 * t + 8, :], tsh_ref[8 * t : 8 * t + 8, :]) for t in range(2)]
                    for v in (x0, x1, xh)
                ]

                def mix(j, k):
                    return bw_ref[j, k, 0] * acts[k][0] + bw_ref[j, k, 1] * acts[k][1]

                blend_ref[1, r + 1, 0:8, :] = mix(1, 0)
                blend_ref[1, r + 1, 8:16, :] = mix(1, 1)
                f = [pltpu.roll(mix(2, k), 7, 0) for k in range(3)]
                blend_ref[2, r + 1, 0:8, :] = jnp.where(sub_id < 7, f[0], f[1])
                blend_ref[2, r + 1, 8:16, :] = jnp.where(sub_id < 7, f[1], f[2])
                g = [pltpu.roll(mix(0, k), 1, 0) for k in range(3)]
                blend_ref[0, r + 1, 0:8, :] = jnp.where(sub_id > 0, g[0], g[2])
                blend_ref[0, r + 1, 8:16, :] = jnp.where(sub_id > 0, g[1], g[0])
            return carry

        lax.fori_loop(0, rows // 2, activate, 0)

        def gather(r, carry):
            at = pl.ds(pl.multiple_of(r * cols, cols), cols)
            held = None
            for tap in range(9):
                i, j = tap // 3, tap % 3
                v = (
                    blend_ref[j, r + i] + sub_ref[r + DIL * i, 8 * j : 8 * j + cols, :]
                ).astype(BF16)
                a_ref[at, tap * main : (tap + 1) * main] = v[:, :main]
                if rem:
                    base = 9 * main + tap * rem
                    if tap % 2 == 0 and tap < 8:
                        held = v[:, main:]
                    elif tap < 8:
                        a_ref[at, base - rem : base + rem] = jnp.concatenate(
                            [held, v[:, main:]], axis=1
                        )
                    else:
                        a_ref[at, base : base + rem] = v[:, main:]
            return carry

        for c in copies:
            c.wait()
        for m in range(0, rows, 8):
            for r in range(m, m + 8):
                gather(r, 0)
            at = pl.ds(m * cols, 8 * cols)
            acc = jnp.dot(a_ref[at, :], w_ref[...], preferred_element_type=F32)
            o_ref[at, :] = (0.5 * acc + bias).astype(BF16)

    vmem = pl.BlockSpec(memory_space=pltpu.VMEM)
    return pl.pallas_call(
        kernel,
        in_specs=[vmem] * 6 + [pl.BlockSpec(memory_space=pltpu.HBM)],
        out_specs=vmem,
        out_shape=jax.ShapeDtypeStruct((pixels, out_channels), BF16),
        scratch_shapes=[
            pltpu.VMEM((depth, out_channels), BF16),
            pltpu.SemaphoreType.DMA((18,)),
            pltpu.VMEM((pixels, depth), BF16),
            pltpu.VMEM((rows + 2 * DIL, 4 * 8, channels), F32),
            pltpu.VMEM((3, rows + 2, cols, channels), F32),
            pltpu.VMEM((64, channels), F32),
            pltpu.VMEM((64, channels), F32),
            pltpu.VMEM((16, channels), F32),
            pltpu.VMEM((16, channels), F32),
        ],
        compiler_params=pltpu.CompilerParams(vmem_limit_bytes=52 * 2**20),
        name="norm_conv",
    )


def make_local(count):
    def local(latent, gain, shift, weight, bias):
        rows, cols, channels = latent.shape
        out_channels = weight.shape[3]
        stride_blocks = STRIDE // cols
        tiles = -(-(count + (OVER // 2) // cols) // stride_blocks)
        tile_rows = -(-tiles // 8) * 8
        x = latent.reshape(rows * cols, channels)
        stats, edge_a, edge_b, x_near = make_stats(rows, cols, channels, tile_rows)(x)
        pairs_a = [(i, i ^ 1) for i in range(count)]
        pairs_b = []
        for i in range(1, count - 1, 2):
            pairs_b += [(i, i + 1), (i + 1, i)]
        halo_a = lax.ppermute(edge_a, "wide", pairs_a)

        def summed(stats, step):
            return stats + lax.ppermute(stats, "wide", [(i, i ^ step) for i in range(count)])

        spare = jnp.zeros((-channels % 128,), F32)
        vectors = jnp.concatenate([gain, spare, shift, spare, bias, spare])
        step = 1
        while step < count:
            stats = summed(stats, step)
            if step == 2:
                blend, stats = lax.optimization_barrier((blend, stats))
            if step == 1:
                edge_b, stats = lax.optimization_barrier((edge_b, stats))
                halo_b = lax.ppermute(edge_b, "wide", pairs_b)
                blend = make_blend(cols, channels, count)(stats)
            step *= 2
        out = make_main(rows, cols, channels, out_channels, tile_rows, count)(
            x_near, halo_a, halo_b, stats, vectors, blend, weight
        )
        return out.reshape(rows, cols, out_channels)

    return local


def solution(mesh):
    in_specs = (P("img", "wide", None), P(), P(), P(), P())
    out_specs = P("img", "wide", None)
    return jax.shard_map(
        make_local(mesh.shape["wide"]),
        mesh=mesh,
        in_specs=in_specs,
        out_specs=out_specs,
        check_vma=False,
    )
```

```python
import jax
import jax.numpy as jnp
from jax import lax
from jax.experimental import pallas as pl
from jax.experimental.pallas import tpu as pltpu
from jax.sharding import PartitionSpec as P

NORM_GROUPS = 32
TILE = 128
OVER = 32
DIL = 8
STRIDE = 96
EPS = 1e-05
F32 = jnp.float32
BF16 = jnp.bfloat16


def iota(shape, dim):
    return lax.broadcasted_iota(jnp.int32, shape, dim)


def group_onehot(channels, per_group, offset):
    lane = iota((128, channels), 0) - offset
    first = lane * per_group
    ch = iota((128, channels), 1)
    return ((ch >= first) & (ch < first + per_group) & (lane >= 0)).astype(F32)


def group_onehot_t(channels, per_group, offset):
    lane = iota((channels, 128), 1) - offset
    first = lane * per_group
    ch = iota((channels, 128), 0)
    return ((ch >= first) & (ch < first + per_group) & (lane >= 0)).astype(F32)


def make_stats(rows, cols, channels, tile_rows):
    per_group = channels // NORM_GROUPS
    rim_blocks = (OVER // 2) // cols
    stride_blocks = STRIDE // cols
    tile_blocks = TILE // cols

    def kernel(x_ref, stats_ref, ea_ref, eb_ref, near_ref, s_ref, q_ref):
        block = lax.axis_index("wide")
        even = lax.rem(block, 2) == 0
        for a in range(0, DIL, 2):
            s = [jnp.zeros((8, channels), F32) for _ in range(2)]
            q = [jnp.zeros((8, channels), F32) for _ in range(2)]
            for rr in range(rows // DIL):
                pa, pb = [], []
                for u in range(2):
                    r = rr * DIL + a + u
                    x = x_ref[r * cols : (r + 1) * cols, :]
                    near_ref[r * cols : (r + 1) * cols, :] = x
                    x = x.astype(F32)
                    lo, hi = x[:8], x[8:]
                    s[u] += lo + hi
                    q[u] += lo * lo + hi * hi
                    pa.append(jnp.where(even, hi, lo))
                    pb.append(jnp.where(even, lo, hi))
                r0 = (rr * DIL + a) * 8
                ea_ref[r0 : r0 + 16, :] = jnp.concatenate(pa, axis=0).astype(BF16)
                eb_ref[r0 : r0 + 16, :] = jnp.concatenate(pb, axis=0).astype(BF16)
            for u in range(2):
                s_ref[(a + u) * 8 : (a + u) * 8 + 8, :] = s[u]
                q_ref[(a + u) * 8 : (a + u) * 8 + 8, :] = q[u]
        total = None
        for ref, half, offset in (
            (s_ref, 0, 0),
            (s_ref, 1, 32),
            (q_ref, 0, 64),
            (q_ref, 1, 96),
        ):
            term = jnp.dot(
                ref[half * 32 : half * 32 + 32, :],
                group_onehot_t(channels, per_group, offset),
                precision=lax.Precision.HIGHEST,
                preferred_element_type=F32,
            )
            total = term if total is None else total + term
        stats_ref[0:32, :] = total
        line = jnp.sum(total, axis=0, keepdims=True)
        line = jnp.broadcast_to(line, (8, 128))
        line = line + pltpu.roll(line, 96, 1)
        for k in range(tile_rows // 8):
            start = (iota((8, 128), 0) + 8 * k) * stride_blocks - rim_blocks
            covers = (block >= start) & (block < start + tile_blocks)
            stats_ref[32 + 8 * k : 40 + 8 * k, :] = jnp.where(covers, line, 0.0)

    return pl.pallas_call(
        kernel,
        out_shape=(
            jax.ShapeDtypeStruct((32 + tile_rows, 128), F32),
            jax.ShapeDtypeStruct((rows * 8, channels), BF16),
            jax.ShapeDtypeStruct((rows * 8, channels), BF16),
            jax.ShapeDtypeStruct((rows * cols, channels), BF16),
        ),
        scratch_shapes=[
            pltpu.VMEM((64, channels), F32),
            pltpu.VMEM((64, channels), F32),
        ],
        compiler_params=pltpu.CompilerParams(vmem_limit_bytes=16 * 2**20),
        name="block_stats",
    )


def make_blend(cols, channels, count):
    rim = OVER // 2

    def kernel(after_ref, bw_ref):
        block = lax.axis_index("wide")
        tile0 = lax.div(block + rim // cols, STRIDE // cols)
        tile1 = tile0 - 1
        sub_id = iota((8, channels), 0)
        for k in range(3):
            if k < 2:
                col = sub_id + 8 * k
            else:
                col = jnp.where(sub_id < 4, sub_id + cols, sub_id - 8)
            col = col + block * cols
            in_image = (col >= 0) & (col < count * cols)
            for j in range(3):
                out_col = col - (j - 1)
                ramps = []
                for tid in (tile0, tile1):
                    q = out_col - (tid * STRIDE - rim)
                    ok = (q >= 0) & (q < TILE) & (tid >= 0)
                    ramp = jnp.minimum(q + 1, TILE - q).astype(F32)
                    ramps.append(jnp.where(ok, ramp, 0.0))
                whole = jnp.maximum(ramps[0] + ramps[1], 1.0)
                for t, tid in enumerate((tile0, tile1)):
                    q = col - (tid * STRIDE - rim)
                    ok = (q >= 0) & (q < TILE) & in_image
                    bw_ref[j, k, t] = jnp.where(ok, ramps[t] / whole, 0.0)


    return pl.pallas_call(
        kernel,
        in_specs=[pl.BlockSpec(memory_space=pl.ANY)],
        out_specs=pl.BlockSpec(memory_space=pltpu.VMEM),
        out_shape=jax.ShapeDtypeStruct((3, 3, 2, 8, channels), F32),
        compiler_params=pltpu.CompilerParams(vmem_limit_bytes=16 * 2**20),
        cost_estimate=pl.CostEstimate(flops=5000000000, bytes_accessed=0, transcendentals=0),
        name="blend_weights",
    )


def make_weights(channels, out_channels):
    main = (channels // 128) * 128
    rem = channels - main

    def kernel(after_ref, w_hbm, w_ref, sem):
        copies = []
        for tap in range(9):
            i, j = tap // 3, tap % 3
            copies.append(
                pltpu.make_async_copy(
                    w_hbm.at[i, j, pl.ds(0, main), :],
                    w_ref.at[pl.ds(tap * main, main), :],
                    sem.at[2 * tap],
                )
            )
            copies.append(
                pltpu.make_async_copy(
                    w_hbm.at[i, j, pl.ds(main, rem), :],
                    w_ref.at[pl.ds(9 * main + tap * rem, rem), :],
                    sem.at[2 * tap + 1],
                )
            )
        for c in copies:
            c.start()

        for c in copies:
            c.wait()

    return pl.pallas_call(
        kernel,
        in_specs=[pl.BlockSpec(memory_space=pl.ANY), pl.BlockSpec(memory_space=pltpu.HBM)],
        out_specs=pl.BlockSpec(memory_space=pltpu.VMEM),
        out_shape=jax.ShapeDtypeStruct((9 * channels, out_channels), BF16),
        scratch_shapes=[pltpu.SemaphoreType.DMA((18,))],
        compiler_params=pltpu.CompilerParams(vmem_limit_bytes=50 * 2**20),
        cost_estimate=pl.CostEstimate(flops=5 * 10**9, bytes_accessed=0, transcendentals=0),
        name="conv_weights",
    )


def make_main(rows, cols, channels, out_channels, tile_rows, count):
    per_group = channels // NORM_GROUPS
    rim = OVER // 2
    rim_blocks = rim // cols
    stride_blocks = STRIDE // cols
    tile_blocks = TILE // cols
    pixels = rows * cols
    main = (channels // 128) * 128
    rem = channels - main
    depth = 9 * channels
    sub_items = float((rows // DIL) * (cols // DIL) * count * per_group)
    all_rows = 32 + tile_rows

    def kernel(
        x_ref, ha_ref, hb_ref, stats_ref, vec_ref, bw_ref, w_ref, o_ref,
        a_ref, sub_ref, blend_ref, sc_ref, sh_ref, tsc_ref, tsh_ref,
    ):
        block = lax.axis_index("wide")
        even = lax.rem(block, 2) == 0
        tile0 = lax.div(block + rim_blocks, stride_blocks)
        tile1 = tile0 - 1

        stats = stats_ref[...]
        row_id = iota((all_rows, 128), 0)
        lane_id = iota((all_rows, 128), 1)
        start = (row_id - 32) * stride_blocks - rim_blocks
        blocks = jnp.minimum(start + tile_blocks, count) - jnp.maximum(start, 0)
        tile_items = jnp.maximum(blocks, 1).astype(F32) * float(pixels * per_group)
        is_sub = row_id < 32
        items = jnp.where(is_sub, sub_items, tile_items)
        mean = stats / items
        square = pltpu.roll(stats, 64, 1) / items
        inverse = lax.rsqrt(square - mean * mean + EPS)
        valid = lane_id < jnp.where(is_sub, 64, 32)
        mean = jnp.where(valid, mean, 0.0)
        inverse = jnp.where(valid, inverse, 0.0)
        both = jnp.concatenate([mean, inverse], axis=0)
        vec = vec_ref[...].reshape(1, -1)
        wide_c = vec.shape[1] // 3
        gain = 0.5 * vec[:, :channels]
        shift = 0.5 * vec[:, wide_c : wide_c + channels]
        bias = vec[:, 2 * wide_c : 2 * wide_c + channels]
        for half in range(2):
            wide = jnp.dot(
                both,
                group_onehot(channels, per_group, 32 * half),
                precision=lax.Precision.HIGHEST,
                preferred_element_type=F32,
            )
            scale = wide[all_rows:] * gain
            offset = shift - wide[:all_rows] * scale
            sc_ref[32 * half : 32 * half + 32, :] = scale[:32]
            sh_ref[32 * half : 32 * half + 32, :] = offset[:32]
            if half == 0:
                tile_row = iota((tile_rows, channels), 0)
                for t, tid in enumerate((tile0, tile1)):
                    pick = tile_row == jnp.maximum(tid, 0)
                    for ref, values in ((tsc_ref, scale), (tsh_ref, offset)):
                        line = jnp.sum(
                            jnp.where(pick, values[32:], 0.0), axis=0, keepdims=True
                        )
                        ref[8 * t : 8 * t + 8, :] = jnp.broadcast_to(line, (8, channels))

        left_ok = jnp.where(block > 0, 1.0, 0.0).astype(F32)
        right_ok = jnp.where(block < count - 1, 1.0, 0.0).astype(F32)

        sub_id = iota((8, channels), 0)
        def silu(x, scale, offset):
            h = x * scale + offset
            return h + h * jnp.tanh(h)

        def activate(m, tiles):
            ha = ha_ref[pl.ds(pl.multiple_of(16 * m, 16), 16), :].astype(F32)
            hb = hb_ref[pl.ds(pl.multiple_of(16 * m, 16), 16), :].astype(F32)
            left = jnp.where(even, hb, ha)
            right = jnp.where(even, ha, hb)
            for u in range(2):
                r = 2 * m + u
                x = x_ref[pl.ds(pl.multiple_of(r * cols, cols), cols), :].astype(F32)
                xl, xr = left[8 * u : 8 * u + 8], right[8 * u : 8 * u + 8]
                x0, x1 = x[:8], x[8:]
                res = pl.multiple_of(lax.rem(r, DIL) * 8, 8)
                scale = sc_ref[pl.ds(res, 8), :]
                offset = sh_ref[pl.ds(res, 8), :]
                sub_ref[r, 0:8, :] = silu(xl, scale, offset) * left_ok
                sub_ref[r, 8:16, :] = silu(x0, scale, offset)
                sub_ref[r, 16:24, :] = silu(x1, scale, offset)
                sub_ref[r, 24:32, :] = silu(xr, scale, offset) * right_ok
                xh = jnp.where(sub_id < 4, xr, xl)
                acts = [
                    [
                        silu(v, tsc_ref[8 * t : 8 * t + 8, :], tsh_ref[8 * t : 8 * t + 8, :])
                        for t in range(tiles)
                    ]
                    for v in (x0, x1, xh)
                ]

                def mix(j, k):
                    if tiles == 1:
                        return acts[k][0] if k < 2 else acts[k][0] * rim_ok
                    return bw_ref[j, k, 0] * acts[k][0] + bw_ref[j, k, 1] * acts[k][1]

                blend_ref[1, r, 0:8, :] = mix(1, 0)
                blend_ref[1, r, 8:16, :] = mix(1, 1)
                f = [pltpu.roll(mix(2, k), 7, 0) for k in range(3)]
                blend_ref[2, r, 0:8, :] = jnp.where(sub_id < 7, f[0], f[1])
                blend_ref[2, r, 8:16, :] = jnp.where(sub_id < 7, f[1], f[2])
                g = [pltpu.roll(mix(0, k), 1, 0) for k in range(3)]
                blend_ref[0, r, 0:8, :] = jnp.where(sub_id > 0, g[0], g[2])
                blend_ref[0, r, 8:16, :] = jnp.where(sub_id > 0, g[1], g[0])

        rim_col = jnp.where(sub_id < 4, sub_id + cols, sub_id - 8) + block * cols
        rim_at = rim_col - (tile0 * STRIDE - rim)
        rim_in = (rim_at >= 0) & (rim_at < TILE) & (rim_col >= 0) & (rim_col < count * cols)
        rim_ok = jnp.where(rim_in, 1.0, 0.0).astype(F32)
        shared = (tile1 >= 0) & (block < tile1 * stride_blocks - rim_blocks + tile_blocks)

        @pl.when(shared)
        def _():
            @pl.loop(0, rows // 2, unroll=2)
            def _(m):
                activate(m, 2)

        @pl.when(jnp.logical_not(shared))
        def _():
            @pl.loop(0, rows // 2, unroll=2)
            def _(m):
                activate(m, 1)

        def gather(r):
            at = pl.ds(r * cols, cols)
            held = None
            for tap in range(9):
                i, j = tap // 3, tap % 3
                near, far = r + i - 1, r + DIL * (i - 1)
                v = None
                if 0 <= near < rows:
                    v = blend_ref[j, near]
                if 0 <= far < rows:
                    w = sub_ref[far, 8 * j : 8 * j + cols, :]
                    v = w if v is None else v + w
                if v is None:
                    v = jnp.zeros((cols, channels), F32)
                v = v.astype(BF16)
                a_ref[at, tap * main : (tap + 1) * main] = v[:, :main]
                if rem:
                    base = 9 * main + tap * rem
                    if tap % 2 == 0 and tap < 8:
                        held = v[:, main:]
                    elif tap < 8:
                        a_ref[at, base - rem : base + rem] = jnp.concatenate(
                            [held, v[:, main:]], axis=1
                        )
                    else:
                        a_ref[at, base : base + rem] = v[:, main:]

        for m in range(0, rows, 8):
            for r in range(m, m + 8):
                gather(r)
            at = pl.ds(m * cols, 8 * cols)
            acc = jnp.dot(a_ref[at, :], w_ref[...], preferred_element_type=F32)
            o_ref[at, :] = (0.5 * acc + bias).astype(BF16)

    vmem = pl.BlockSpec(memory_space=pltpu.VMEM)
    return pl.pallas_call(
        kernel,
        in_specs=[vmem] * 7,
        out_specs=vmem,
        out_shape=jax.ShapeDtypeStruct((pixels, out_channels), BF16),
        scratch_shapes=[
            pltpu.VMEM((pixels, depth), BF16),
            pltpu.VMEM((rows, 4 * 8, channels), F32),
            pltpu.VMEM((3, rows, cols, channels), F32),
            pltpu.VMEM((64, channels), F32),
            pltpu.VMEM((64, channels), F32),
            pltpu.VMEM((16, channels), F32),
            pltpu.VMEM((16, channels), F32),
        ],
        compiler_params=pltpu.CompilerParams(vmem_limit_bytes=40 * 2**20),
        name="norm_conv",
    )


def make_local(count):
    def local(latent, gain, shift, weight, bias):
        rows, cols, channels = latent.shape
        out_channels = weight.shape[3]
        stride_blocks = STRIDE // cols
        tiles = -(-(count + (OVER // 2) // cols) // stride_blocks)
        tile_rows = -(-tiles // 8) * 8
        x = latent.reshape(rows * cols, channels)
        stats, edge_a, edge_b, x_near = make_stats(rows, cols, channels, tile_rows)(x)
        pairs_a = [(i, i ^ 1) for i in range(count)]
        pairs_b = []
        for i in range(1, count - 1, 2):
            pairs_b += [(i, i + 1), (i + 1, i)]
        halo_a = lax.ppermute(edge_a, "wide", pairs_a)

        def summed(stats, step):
            return stats + lax.ppermute(stats, "wide", [(i, i ^ step) for i in range(count)])

        spare = jnp.zeros((-channels % 128,), F32)
        vectors = jnp.concatenate([gain, spare, shift, spare, bias, spare])
        taps = None
        step = 1
        while step < count:
            stats = summed(stats, step)
            if step == 2:
                blend, stats = lax.optimization_barrier((blend, stats))
            if step == 1:
                edge_b, stats = lax.optimization_barrier((edge_b, stats))
                halo_b = lax.ppermute(edge_b, "wide", pairs_b)
                blend = make_blend(cols, channels, count)(stats)
            step *= 2
            if step == 4 or (taps is None and step >= count):
                taps = make_weights(channels, out_channels)(stats, weight)
            if step == 8:
                taps, stats = lax.optimization_barrier((taps, stats))
        out = make_main(rows, cols, channels, out_channels, tile_rows, count)(
            x_near, halo_a, halo_b, stats, vectors, blend, taps
        )
        return out.reshape(rows, cols, out_channels)

    return local


def solution(mesh):
    in_specs = (P("img", "wide", None), P(), P(), P(), P())
    out_specs = P("img", "wide", None)
    return jax.shard_map(
        make_local(mesh.shape["wide"]),
        mesh=mesh,
        in_specs=in_specs,
        out_specs=out_specs,
        check_vma=False,
    )
```

```python
import jax
import jax.numpy as jnp
from jax import lax
from jax.experimental import pallas as pl
from jax.experimental.pallas import tpu as pltpu
from jax.sharding import PartitionSpec as P

NORM_GROUPS = 32
TILE = 128
OVER = 32
DIL = 8
STRIDE = 96
EPS = 1e-05
F32 = jnp.float32
BF16 = jnp.bfloat16


def iota(shape, dim):
    return lax.broadcasted_iota(jnp.int32, shape, dim)


def group_onehot(channels, per_group, offset):
    lane = iota((128, channels), 0) - offset
    first = lane * per_group
    ch = iota((128, channels), 1)
    return ((ch >= first) & (ch < first + per_group) & (lane >= 0)).astype(F32)


def group_onehot_t(channels, per_group, offset):
    lane = iota((channels, 128), 1) - offset
    first = lane * per_group
    ch = iota((channels, 128), 0)
    return ((ch >= first) & (ch < first + per_group) & (lane >= 0)).astype(F32)


def make_stats(rows, cols, channels, tile_rows):
    per_group = channels // NORM_GROUPS
    rim_blocks = (OVER // 2) // cols
    stride_blocks = STRIDE // cols
    tile_blocks = TILE // cols

    def kernel(x_ref, stats_ref, ea_ref, eb_ref, near_ref, s_ref, q_ref):
        block = lax.axis_index("wide")
        even = lax.rem(block, 2) == 0
        for a in range(0, DIL, 2):
            s = [jnp.zeros((8, channels), F32) for _ in range(2)]
            q = [jnp.zeros((8, channels), F32) for _ in range(2)]
            for rr in range(rows // DIL):
                pa, pb = [], []
                for u in range(2):
                    r = rr * DIL + a + u
                    x = x_ref[r * cols : (r + 1) * cols, :]
                    near_ref[r * cols : (r + 1) * cols, :] = x
                    x = x.astype(F32)
                    lo, hi = x[:8], x[8:]
                    s[u] += lo + hi
                    q[u] += lo * lo + hi * hi
                    pa.append(jnp.where(even, hi, lo))
                    pb.append(jnp.where(even, lo, hi))
                r0 = (rr * DIL + a) * 8
                ea_ref[r0 : r0 + 16, :] = jnp.concatenate(pa, axis=0).astype(BF16)
                eb_ref[r0 : r0 + 16, :] = jnp.concatenate(pb, axis=0).astype(BF16)
            for u in range(2):
                s_ref[(a + u) * 8 : (a + u) * 8 + 8, :] = s[u]
                q_ref[(a + u) * 8 : (a + u) * 8 + 8, :] = q[u]
        total = None
        for ref, half, offset in (
            (s_ref, 0, 0),
            (s_ref, 1, 32),
            (q_ref, 0, 64),
            (q_ref, 1, 96),
        ):
            term = jnp.dot(
                ref[half * 32 : half * 32 + 32, :],
                group_onehot_t(channels, per_group, offset),
                precision=lax.Precision.HIGHEST,
                preferred_element_type=F32,
            )
            total = term if total is None else total + term
        stats_ref[0:32, :] = total
        line = jnp.sum(total, axis=0, keepdims=True)
        line = jnp.broadcast_to(line, (8, 128))
        line = line + pltpu.roll(line, 96, 1)
        for k in range(tile_rows // 8):
            start = (iota((8, 128), 0) + 8 * k) * stride_blocks - rim_blocks
            covers = (block >= start) & (block < start + tile_blocks)
            stats_ref[32 + 8 * k : 40 + 8 * k, :] = jnp.where(covers, line, 0.0)

    return pl.pallas_call(
        kernel,
        out_shape=(
            jax.ShapeDtypeStruct((32 + tile_rows, 128), F32),
            jax.ShapeDtypeStruct((rows * 8, channels), BF16),
            jax.ShapeDtypeStruct((rows * 8, channels), BF16),
            jax.ShapeDtypeStruct((rows * cols, channels), BF16),
        ),
        scratch_shapes=[
            pltpu.VMEM((64, channels), F32),
            pltpu.VMEM((64, channels), F32),
        ],
        compiler_params=pltpu.CompilerParams(vmem_limit_bytes=16 * 2**20),
        name="block_stats",
    )


def make_blend(cols, channels, count):
    rim = OVER // 2

    def kernel(after_ref, bw_ref):
        block = lax.axis_index("wide")
        tile0 = lax.div(block + rim // cols, STRIDE // cols)
        tile1 = tile0 - 1
        sub_id = iota((8, channels), 0)
        for k in range(3):
            if k < 2:
                col = sub_id + 8 * k
            else:
                col = jnp.where(sub_id < 4, sub_id + cols, sub_id - 8)
            col = col + block * cols
            in_image = (col >= 0) & (col < count * cols)
            for j in range(3):
                out_col = col - (j - 1)
                ramps = []
                for tid in (tile0, tile1):
                    q = out_col - (tid * STRIDE - rim)
                    ok = (q >= 0) & (q < TILE) & (tid >= 0)
                    ramp = jnp.minimum(q + 1, TILE - q).astype(F32)
                    ramps.append(jnp.where(ok, ramp, 0.0))
                whole = jnp.maximum(ramps[0] + ramps[1], 1.0)
                for t, tid in enumerate((tile0, tile1)):
                    q = col - (tid * STRIDE - rim)
                    ok = (q >= 0) & (q < TILE) & in_image
                    bw_ref[j, k, t] = jnp.where(ok, ramps[t] / whole, 0.0)


    return pl.pallas_call(
        kernel,
        in_specs=[pl.BlockSpec(memory_space=pl.ANY)],
        out_specs=pl.BlockSpec(memory_space=pltpu.VMEM),
        out_shape=jax.ShapeDtypeStruct((3, 3, 2, 8, channels), F32),
        compiler_params=pltpu.CompilerParams(vmem_limit_bytes=16 * 2**20),
        cost_estimate=pl.CostEstimate(flops=5000000000, bytes_accessed=0, transcendentals=0),
        name="blend_weights",
    )


def make_weights(channels, out_channels):
    main = (channels // 128) * 128
    rem = channels - main

    def kernel(after_ref, w_hbm, w_ref, sem):
        copies = []
        for tap in range(9):
            i, j = tap // 3, tap % 3
            copies.append(
                pltpu.make_async_copy(
                    w_hbm.at[i, j, pl.ds(0, main), :],
                    w_ref.at[pl.ds(tap * main, main), :],
                    sem.at[2 * tap],
                )
            )
            copies.append(
                pltpu.make_async_copy(
                    w_hbm.at[i, j, pl.ds(main, rem), :],
                    w_ref.at[pl.ds(9 * main + tap * rem, rem), :],
                    sem.at[2 * tap + 1],
                )
            )
        for c in copies:
            c.start()

        for c in copies:
            c.wait()

    return pl.pallas_call(
        kernel,
        in_specs=[pl.BlockSpec(memory_space=pl.ANY), pl.BlockSpec(memory_space=pltpu.HBM)],
        out_specs=pl.BlockSpec(memory_space=pltpu.VMEM),
        out_shape=jax.ShapeDtypeStruct((9 * channels, out_channels), BF16),
        scratch_shapes=[pltpu.SemaphoreType.DMA((18,))],
        compiler_params=pltpu.CompilerParams(vmem_limit_bytes=50 * 2**20),
        cost_estimate=pl.CostEstimate(flops=5 * 10**9, bytes_accessed=0, transcendentals=0),
        name="conv_weights",
    )


def make_main(rows, cols, channels, out_channels, tile_rows, count):
    per_group = channels // NORM_GROUPS
    rim = OVER // 2
    rim_blocks = rim // cols
    stride_blocks = STRIDE // cols
    tile_blocks = TILE // cols
    pixels = rows * cols
    main = (channels // 128) * 128
    rem = channels - main
    depth = 9 * channels
    sub_items = float((rows // DIL) * (cols // DIL) * count * per_group)
    all_rows = 32 + tile_rows

    def kernel(
        x_ref, ha_ref, hb_ref, stats_ref, vec_ref, bw_ref, w_ref, o_ref,
        a_ref, sub_ref, blend_ref, sc_ref, sh_ref, tsc_ref, tsh_ref,
    ):
        block = lax.axis_index("wide")
        even = lax.rem(block, 2) == 0
        tile0 = lax.div(block + rim_blocks, stride_blocks)
        tile1 = tile0 - 1

        stats = stats_ref[...]
        row_id = iota((all_rows, 128), 0)
        lane_id = iota((all_rows, 128), 1)
        start = (row_id - 32) * stride_blocks - rim_blocks
        blocks = jnp.minimum(start + tile_blocks, count) - jnp.maximum(start, 0)
        tile_items = jnp.maximum(blocks, 1).astype(F32) * float(pixels * per_group)
        is_sub = row_id < 32
        items = jnp.where(is_sub, sub_items, tile_items)
        mean = stats / items
        square = pltpu.roll(stats, 64, 1) / items
        inverse = lax.rsqrt(square - mean * mean + EPS)
        valid = lane_id < jnp.where(is_sub, 64, 32)
        mean = jnp.where(valid, mean, 0.0)
        inverse = jnp.where(valid, inverse, 0.0)
        both = jnp.concatenate([mean, inverse], axis=0)
        vec = vec_ref[...].reshape(1, -1)
        wide_c = vec.shape[1] // 3
        gain = 0.5 * vec[:, :channels]
        shift = 0.5 * vec[:, wide_c : wide_c + channels]
        bias = vec[:, 2 * wide_c : 2 * wide_c + channels]
        for half in range(2):
            wide = jnp.dot(
                both,
                group_onehot(channels, per_group, 32 * half),
                precision=lax.Precision.HIGHEST,
                preferred_element_type=F32,
            )
            scale = wide[all_rows:] * gain
            offset = shift - wide[:all_rows] * scale
            sc_ref[32 * half : 32 * half + 32, :] = scale[:32]
            sh_ref[32 * half : 32 * half + 32, :] = offset[:32]
            if half == 0:
                tile_row = iota((tile_rows, channels), 0)
                for t, tid in enumerate((tile0, tile1)):
                    pick = tile_row == jnp.maximum(tid, 0)
                    for ref, values in ((tsc_ref, scale), (tsh_ref, offset)):
                        line = jnp.sum(
                            jnp.where(pick, values[32:], 0.0), axis=0, keepdims=True
                        )
                        ref[8 * t : 8 * t + 8, :] = jnp.broadcast_to(line, (8, channels))

        left_ok = jnp.where(block > 0, 1.0, 0.0).astype(F32)
        right_ok = jnp.where(block < count - 1, 1.0, 0.0).astype(F32)

        sub_id = iota((8, channels), 0)
        def silu(x, scale, offset):
            h = x * scale + offset
            return h + h * jnp.tanh(h)

        def activate(m, tiles):
            ha = ha_ref[pl.ds(pl.multiple_of(16 * m, 16), 16), :].astype(F32)
            hb = hb_ref[pl.ds(pl.multiple_of(16 * m, 16), 16), :].astype(F32)
            left = jnp.where(even, hb, ha)
            right = jnp.where(even, ha, hb)
            for u in range(2):
                r = 2 * m + u
                x = x_ref[pl.ds(pl.multiple_of(r * cols, cols), cols), :].astype(F32)
                xl, xr = left[8 * u : 8 * u + 8], right[8 * u : 8 * u + 8]
                x0, x1 = x[:8], x[8:]
                res = pl.multiple_of(lax.rem(r, DIL) * 8, 8)
                scale = sc_ref[pl.ds(res, 8), :]
                offset = sh_ref[pl.ds(res, 8), :]
                sub_ref[r, 0:8, :] = silu(xl, scale, offset) * left_ok
                sub_ref[r, 8:16, :] = silu(x0, scale, offset)
                sub_ref[r, 16:24, :] = silu(x1, scale, offset)
                sub_ref[r, 24:32, :] = silu(xr, scale, offset) * right_ok
                xh = jnp.where(sub_id < 4, xr, xl)
                acts = [
                    [
                        silu(v, tsc_ref[8 * t : 8 * t + 8, :], tsh_ref[8 * t : 8 * t + 8, :])
                        for t in range(tiles)
                    ]
                    for v in (x0, x1, xh)
                ]

                def mix(j, k):
                    if tiles == 1:
                        return acts[k][0] if k < 2 else acts[k][0] * rim_ok
                    return bw_ref[j, k, 0] * acts[k][0] + bw_ref[j, k, 1] * acts[k][1]

                blend_ref[1, r, 0:8, :] = mix(1, 0)
                blend_ref[1, r, 8:16, :] = mix(1, 1)
                f = [pltpu.roll(mix(2, k), 7, 0) for k in range(3)]
                blend_ref[2, r, 0:8, :] = jnp.where(sub_id < 7, f[0], f[1])
                blend_ref[2, r, 8:16, :] = jnp.where(sub_id < 7, f[1], f[2])
                g = [pltpu.roll(mix(0, k), 1, 0) for k in range(3)]
                blend_ref[0, r, 0:8, :] = jnp.where(sub_id > 0, g[0], g[2])
                blend_ref[0, r, 8:16, :] = jnp.where(sub_id > 0, g[1], g[0])

        rim_col = jnp.where(sub_id < 4, sub_id + cols, sub_id - 8) + block * cols
        rim_at = rim_col - (tile0 * STRIDE - rim)
        rim_in = (rim_at >= 0) & (rim_at < TILE) & (rim_col >= 0) & (rim_col < count * cols)
        rim_ok = jnp.where(rim_in, 1.0, 0.0).astype(F32)
        shared = (tile1 >= 0) & (block < tile1 * stride_blocks - rim_blocks + tile_blocks)

        @pl.when(shared)
        def _():
            @pl.loop(0, rows // 2, unroll=2)
            def _(m):
                activate(m, 2)

        @pl.when(jnp.logical_not(shared))
        def _():
            @pl.loop(0, rows // 2, unroll=2)
            def _(m):
                activate(m, 1)

        def gather(r):
            at = pl.ds(r * cols, cols)
            held = None
            for tap in range(9):
                i, j = tap // 3, tap % 3
                near, far = r + i - 1, r + DIL * (i - 1)
                v = None
                if 0 <= near < rows:
                    v = blend_ref[j, near]
                if 0 <= far < rows:
                    w = sub_ref[far, 8 * j : 8 * j + cols, :]
                    v = w if v is None else v + w
                if v is None:
                    v = jnp.zeros((cols, channels), F32)
                v = v.astype(BF16)
                a_ref[at, tap * main : (tap + 1) * main] = v[:, :main]
                if rem:
                    base = 9 * main + tap * rem
                    if tap % 2 == 0 and tap < 8:
                        held = v[:, main:]
                    elif tap < 8:
                        a_ref[at, base - rem : base + rem] = jnp.concatenate(
                            [held, v[:, main:]], axis=1
                        )
                    else:
                        a_ref[at, base : base + rem] = v[:, main:]

        for m in range(0, rows, 8):
            for r in range(m, m + 8):
                gather(r)
            at = pl.ds(m * cols, 8 * cols)
            acc = jnp.dot(a_ref[at, :], w_ref[...], preferred_element_type=F32)
            o_ref[at, :] = (0.5 * acc + bias).astype(BF16)

    vmem = pl.BlockSpec(memory_space=pltpu.VMEM)
    return pl.pallas_call(
        kernel,
        in_specs=[vmem] * 7,
        out_specs=vmem,
        out_shape=jax.ShapeDtypeStruct((pixels, out_channels), BF16),
        scratch_shapes=[
            pltpu.VMEM((pixels, depth), BF16),
            pltpu.VMEM((rows, 4 * 8, channels), F32),
            pltpu.VMEM((3, rows, cols, channels), F32),
            pltpu.VMEM((64, channels), F32),
            pltpu.VMEM((64, channels), F32),
            pltpu.VMEM((16, channels), F32),
            pltpu.VMEM((16, channels), F32),
        ],
        compiler_params=pltpu.CompilerParams(vmem_limit_bytes=40 * 2**20),
        name="norm_conv",
    )


def make_local(count):
    def local(latent, gain, shift, weight, bias):
        rows, cols, channels = latent.shape
        out_channels = weight.shape[3]
        stride_blocks = STRIDE // cols
        tiles = -(-(count + (OVER // 2) // cols) // stride_blocks)
        tile_rows = -(-tiles // 8) * 8
        x = latent.reshape(rows * cols, channels)
        stats, edge_a, edge_b, x_near = make_stats(rows, cols, channels, tile_rows)(x)
        pairs_a = [(i, i ^ 1) for i in range(count)]
        pairs_b = []
        for i in range(1, count - 1, 2):
            pairs_b += [(i, i + 1), (i + 1, i)]
        halo_a = lax.ppermute(edge_a, "wide", pairs_a)

        def summed(stats, step):
            mask = step + 1 if 1 < step < 8 else step
            return stats + lax.ppermute(stats, "wide", [(i, i ^ mask) for i in range(count)])

        spare = jnp.zeros((-channels % 128,), F32)
        vectors = jnp.concatenate([gain, spare, shift, spare, bias, spare])
        taps = None
        step = 1
        while step < count:
            stats = summed(stats, step)
            if step == 2:
                blend, stats = lax.optimization_barrier((blend, stats))
            if step == 1:
                edge_b, stats = lax.optimization_barrier((edge_b, stats))
                halo_b = lax.ppermute(edge_b, "wide", pairs_b)
                blend = make_blend(cols, channels, count)(stats)
            step *= 2
            if step == 4 or (taps is None and step >= count):
                taps = make_weights(channels, out_channels)(stats, weight)
            if step == 8:
                taps, stats = lax.optimization_barrier((taps, stats))
        out = make_main(rows, cols, channels, out_channels, tile_rows, count)(
            x_near, halo_a, halo_b, stats, vectors, blend, taps
        )
        return out.reshape(rows, cols, out_channels)

    return local


def solution(mesh):
    in_specs = (P("img", "wide", None), P(), P(), P(), P())
    out_specs = P("img", "wide", None)
    return jax.shard_map(
        make_local(mesh.shape["wide"]),
        mesh=mesh,
        in_specs=in_specs,
        out_specs=out_specs,
        check_vma=False,
    )
```

```python
import jax
import jax.numpy as jnp
from jax import lax
from jax.experimental import pallas as pl
from jax.experimental.pallas import tpu as pltpu
from jax.sharding import PartitionSpec as P

NORM_GROUPS = 32
TILE = 128
OVER = 32
DIL = 8
STRIDE = 96
EPS = 1e-05
F32 = jnp.float32
BF16 = jnp.bfloat16


def iota(shape, dim):
    return lax.broadcasted_iota(jnp.int32, shape, dim)


def group_onehot(channels, per_group, offset):
    lane = iota((128, channels), 0) - offset
    first = lane * per_group
    ch = iota((128, channels), 1)
    return ((ch >= first) & (ch < first + per_group) & (lane >= 0)).astype(F32)


def group_onehot_t(channels, per_group, offset):
    lane = iota((channels, 128), 1) - offset
    first = lane * per_group
    ch = iota((channels, 128), 0)
    return ((ch >= first) & (ch < first + per_group) & (lane >= 0)).astype(F32)


def make_stats(rows, cols, channels, tile_rows):
    per_group = channels // NORM_GROUPS
    rim_blocks = (OVER // 2) // cols
    stride_blocks = STRIDE // cols
    tile_blocks = TILE // cols

    def kernel(x_ref, stats_ref, ea_ref, eb_ref, near_ref, s_ref, q_ref):
        block = lax.axis_index("wide")
        even = lax.rem(block, 2) == 0
        for a in range(0, DIL, 2):
            s = [jnp.zeros((8, channels), F32) for _ in range(2)]
            q = [jnp.zeros((8, channels), F32) for _ in range(2)]
            for rr in range(rows // DIL):
                pa, pb = [], []
                for u in range(2):
                    r = rr * DIL + a + u
                    x = x_ref[r * cols : (r + 1) * cols, :]
                    near_ref[r * cols : (r + 1) * cols, :] = x
                    x = x.astype(F32)
                    lo, hi = x[:8], x[8:]
                    s[u] += lo + hi
                    q[u] += lo * lo + hi * hi
                    pa.append(jnp.where(even, hi, lo))
                    pb.append(jnp.where(even, lo, hi))
                r0 = (rr * DIL + a) * 8
                ea_ref[r0 : r0 + 16, :] = jnp.concatenate(pa, axis=0).astype(BF16)
                eb_ref[r0 : r0 + 16, :] = jnp.concatenate(pb, axis=0).astype(BF16)
            for u in range(2):
                s_ref[(a + u) * 8 : (a + u) * 8 + 8, :] = s[u]
                q_ref[(a + u) * 8 : (a + u) * 8 + 8, :] = q[u]
        total = None
        for ref, half, offset in (
            (s_ref, 0, 0),
            (s_ref, 1, 32),
            (q_ref, 0, 64),
            (q_ref, 1, 96),
        ):
            term = jnp.dot(
                ref[half * 32 : half * 32 + 32, :],
                group_onehot_t(channels, per_group, offset),
                precision=lax.Precision.HIGHEST,
                preferred_element_type=F32,
            )
            total = term if total is None else total + term
        stats_ref[0:32, :] = total
        line = jnp.sum(total, axis=0, keepdims=True)
        line = jnp.broadcast_to(line, (8, 128))
        line = line + pltpu.roll(line, 96, 1)
        for k in range(tile_rows // 8):
            start = (iota((8, 128), 0) + 8 * k) * stride_blocks - rim_blocks
            covers = (block >= start) & (block < start + tile_blocks)
            stats_ref[32 + 8 * k : 40 + 8 * k, :] = jnp.where(covers, line, 0.0)

    return pl.pallas_call(
        kernel,
        out_shape=(
            jax.ShapeDtypeStruct((32 + tile_rows, 128), F32),
            jax.ShapeDtypeStruct((rows * 8, channels), BF16),
            jax.ShapeDtypeStruct((rows * 8, channels), BF16),
            jax.ShapeDtypeStruct((rows * cols, channels), BF16),
        ),
        scratch_shapes=[
            pltpu.VMEM((64, channels), F32),
            pltpu.VMEM((64, channels), F32),
        ],
        compiler_params=pltpu.CompilerParams(vmem_limit_bytes=16 * 2**20),
        name="block_stats",
    )


def make_blend(cols, channels, count):
    rim = OVER // 2

    def kernel(after_ref, bw_ref):
        block = lax.axis_index("wide")
        tile0 = lax.div(block + rim // cols, STRIDE // cols)
        tile1 = tile0 - 1
        sub_id = iota((8, channels), 0)
        for k in range(3):
            if k < 2:
                col = sub_id + 8 * k
            else:
                col = jnp.where(sub_id < 4, sub_id + cols, sub_id - 8)
            col = col + block * cols
            in_image = (col >= 0) & (col < count * cols)
            for j in range(3):
                out_col = col - (j - 1)
                ramps = []
                for tid in (tile0, tile1):
                    q = out_col - (tid * STRIDE - rim)
                    ok = (q >= 0) & (q < TILE) & (tid >= 0)
                    ramp = jnp.minimum(q + 1, TILE - q).astype(F32)
                    ramps.append(jnp.where(ok, ramp, 0.0))
                whole = jnp.maximum(ramps[0] + ramps[1], 1.0)
                for t, tid in enumerate((tile0, tile1)):
                    q = col - (tid * STRIDE - rim)
                    ok = (q >= 0) & (q < TILE) & in_image
                    bw_ref[j, k, t] = jnp.where(ok, ramps[t] / whole, 0.0)


    return pl.pallas_call(
        kernel,
        in_specs=[pl.BlockSpec(memory_space=pl.ANY)],
        out_specs=pl.BlockSpec(memory_space=pltpu.VMEM),
        out_shape=jax.ShapeDtypeStruct((3, 3, 2, 8, channels), F32),
        compiler_params=pltpu.CompilerParams(vmem_limit_bytes=16 * 2**20),
        cost_estimate=pl.CostEstimate(flops=5000000000, bytes_accessed=0, transcendentals=0),
        name="blend_weights",
    )


def make_weights(channels, out_channels):
    main = (channels // 128) * 128
    rem = channels - main

    def kernel(after_ref, w_hbm, w_ref, sem):
        copies = []
        for tap in range(9):
            i, j = tap // 3, tap % 3
            copies.append(
                pltpu.make_async_copy(
                    w_hbm.at[i, j, pl.ds(0, main), :],
                    w_ref.at[pl.ds(tap * main, main), :],
                    sem.at[2 * tap],
                )
            )
            copies.append(
                pltpu.make_async_copy(
                    w_hbm.at[i, j, pl.ds(main, rem), :],
                    w_ref.at[pl.ds(9 * main + tap * rem, rem), :],
                    sem.at[2 * tap + 1],
                )
            )
        for c in copies:
            c.start()

        for c in copies:
            c.wait()

    return pl.pallas_call(
        kernel,
        in_specs=[pl.BlockSpec(memory_space=pl.ANY), pl.BlockSpec(memory_space=pltpu.HBM)],
        out_specs=pl.BlockSpec(memory_space=pltpu.VMEM),
        out_shape=jax.ShapeDtypeStruct((9 * channels, out_channels), BF16),
        scratch_shapes=[pltpu.SemaphoreType.DMA((18,))],
        compiler_params=pltpu.CompilerParams(vmem_limit_bytes=50 * 2**20),
        cost_estimate=pl.CostEstimate(flops=5 * 10**9, bytes_accessed=0, transcendentals=0),
        name="conv_weights",
    )


def make_main(rows, cols, channels, out_channels, tile_rows, count):
    per_group = channels // NORM_GROUPS
    rim = OVER // 2
    rim_blocks = rim // cols
    stride_blocks = STRIDE // cols
    tile_blocks = TILE // cols
    pixels = rows * cols
    main = (channels // 128) * 128
    rem = channels - main
    depth = 9 * channels
    sub_items = float((rows // DIL) * (cols // DIL) * count * per_group)
    all_rows = 32 + tile_rows

    def kernel(
        x_ref, ha_ref, hb_ref, stats_ref, vec_ref, bw_ref, w_ref, o_ref,
        a_ref, sub_ref, blend_ref, sc_ref, sh_ref, tsc_ref, tsh_ref,
    ):
        block = lax.axis_index("wide")
        even = lax.rem(block, 2) == 0
        tile0 = lax.div(block + rim_blocks, stride_blocks)
        tile1 = tile0 - 1

        stats = stats_ref[...]
        row_id = iota((all_rows, 128), 0)
        lane_id = iota((all_rows, 128), 1)
        start = (row_id - 32) * stride_blocks - rim_blocks
        blocks = jnp.minimum(start + tile_blocks, count) - jnp.maximum(start, 0)
        tile_items = jnp.maximum(blocks, 1).astype(F32) * float(pixels * per_group)
        is_sub = row_id < 32
        items = jnp.where(is_sub, sub_items, tile_items)
        mean = stats / items
        square = pltpu.roll(stats, 64, 1) / items
        inverse = lax.rsqrt(square - mean * mean + EPS)
        valid = lane_id < jnp.where(is_sub, 64, 32)
        mean = jnp.where(valid, mean, 0.0)
        inverse = jnp.where(valid, inverse, 0.0)
        both = jnp.concatenate([mean, inverse], axis=0)
        vec = vec_ref[...].reshape(1, -1)
        wide_c = vec.shape[1] // 3
        gain = 0.5 * vec[:, :channels]
        shift = 0.5 * vec[:, wide_c : wide_c + channels]
        bias = vec[:, 2 * wide_c : 2 * wide_c + channels]
        for half in range(2):
            wide = jnp.dot(
                both,
                group_onehot(channels, per_group, 32 * half),
                precision=lax.Precision.HIGHEST,
                preferred_element_type=F32,
            )
            scale = wide[all_rows:] * gain
            offset = shift - wide[:all_rows] * scale
            sc_ref[32 * half : 32 * half + 32, :] = scale[:32]
            sh_ref[32 * half : 32 * half + 32, :] = offset[:32]
            if half == 0:
                tile_row = iota((tile_rows, channels), 0)
                for t, tid in enumerate((tile0, tile1)):
                    pick = tile_row == jnp.maximum(tid, 0)
                    for ref, values in ((tsc_ref, scale), (tsh_ref, offset)):
                        line = jnp.sum(
                            jnp.where(pick, values[32:], 0.0), axis=0, keepdims=True
                        )
                        ref[8 * t : 8 * t + 8, :] = jnp.broadcast_to(line, (8, channels))

        left_ok = jnp.where(block > 0, 1.0, 0.0).astype(F32)
        right_ok = jnp.where(block < count - 1, 1.0, 0.0).astype(F32)

        sub_id = iota((8, channels), 0)
        def silu(x, scale, offset):
            h = x * scale + offset
            return h + h * jnp.tanh(h)

        def activate(m, tiles):
            ha = ha_ref[pl.ds(pl.multiple_of(16 * m, 16), 16), :].astype(F32)
            hb = hb_ref[pl.ds(pl.multiple_of(16 * m, 16), 16), :].astype(F32)
            left = jnp.where(even, hb, ha)
            right = jnp.where(even, ha, hb)
            for u in range(2):
                r = 2 * m + u
                x = x_ref[pl.ds(pl.multiple_of(r * cols, cols), cols), :].astype(F32)
                xl, xr = left[8 * u : 8 * u + 8], right[8 * u : 8 * u + 8]
                x0, x1 = x[:8], x[8:]
                res = pl.multiple_of(lax.rem(r, DIL) * 8, 8)
                scale = sc_ref[pl.ds(res, 8), :]
                offset = sh_ref[pl.ds(res, 8), :]
                sub_ref[r, 0:8, :] = silu(xl, scale, offset) * left_ok
                sub_ref[r, 8:16, :] = silu(x0, scale, offset)
                sub_ref[r, 16:24, :] = silu(x1, scale, offset)
                sub_ref[r, 24:32, :] = silu(xr, scale, offset) * right_ok
                xh = jnp.where(sub_id < 4, xr, xl)
                acts = [
                    [
                        silu(v, tsc_ref[8 * t : 8 * t + 8, :], tsh_ref[8 * t : 8 * t + 8, :])
                        for t in range(tiles)
                    ]
                    for v in (x0, x1, xh)
                ]

                def mix(j, k):
                    if tiles == 1:
                        return acts[k][0] if k < 2 else acts[k][0] * rim_ok
                    return bw_ref[j, k, 0] * acts[k][0] + bw_ref[j, k, 1] * acts[k][1]

                blend_ref[1, r, 0:8, :] = mix(1, 0)
                blend_ref[1, r, 8:16, :] = mix(1, 1)
                f = [pltpu.roll(mix(2, k), 7, 0) for k in range(3)]
                blend_ref[2, r, 0:8, :] = jnp.where(sub_id < 7, f[0], f[1])
                blend_ref[2, r, 8:16, :] = jnp.where(sub_id < 7, f[1], f[2])
                g = [pltpu.roll(mix(0, k), 1, 0) for k in range(3)]
                blend_ref[0, r, 0:8, :] = jnp.where(sub_id > 0, g[0], g[2])
                blend_ref[0, r, 8:16, :] = jnp.where(sub_id > 0, g[1], g[0])

        rim_col = jnp.where(sub_id < 4, sub_id + cols, sub_id - 8) + block * cols
        rim_at = rim_col - (tile0 * STRIDE - rim)
        rim_in = (rim_at >= 0) & (rim_at < TILE) & (rim_col >= 0) & (rim_col < count * cols)
        rim_ok = jnp.where(rim_in, 1.0, 0.0).astype(F32)
        shared = (tile1 >= 0) & (block < tile1 * stride_blocks - rim_blocks + tile_blocks)

        @pl.when(shared)
        def _():
            @pl.loop(0, rows // 2, unroll=2)
            def _(m):
                activate(m, 2)

        @pl.when(jnp.logical_not(shared))
        def _():
            @pl.loop(0, rows // 2, unroll=2)
            def _(m):
                activate(m, 1)

        def gather(r):
            at = pl.ds(r * cols, cols)
            held = None
            for tap in range(9):
                i, j = tap // 3, tap % 3
                near, far = r + i - 1, r + DIL * (i - 1)
                v = None
                if 0 <= near < rows:
                    v = blend_ref[j, near]
                if 0 <= far < rows:
                    w = sub_ref[far, 8 * j : 8 * j + cols, :]
                    v = w if v is None else v + w
                if v is None:
                    v = jnp.zeros((cols, channels), F32)
                v = v.astype(BF16)
                a_ref[at, tap * main : (tap + 1) * main] = v[:, :main]
                if rem:
                    base = 9 * main + tap * rem
                    if tap % 2 == 0 and tap < 8:
                        held = v[:, main:]
                    elif tap < 8:
                        a_ref[at, base - rem : base + rem] = jnp.concatenate(
                            [held, v[:, main:]], axis=1
                        )
                    else:
                        a_ref[at, base : base + rem] = v[:, main:]

        for m in range(0, rows, 8):
            for r in range(m, m + 8):
                gather(r)
            at = pl.ds(m * cols, 8 * cols)
            acc = jnp.dot(a_ref[at, :], w_ref[...], preferred_element_type=F32)
            o_ref[at, :] = (0.5 * acc + bias).astype(BF16)

    vmem = pl.BlockSpec(memory_space=pltpu.VMEM)
    return pl.pallas_call(
        kernel,
        in_specs=[vmem] * 7,
        out_specs=vmem,
        out_shape=jax.ShapeDtypeStruct((pixels, out_channels), BF16),
        scratch_shapes=[
            pltpu.VMEM((pixels, depth), BF16),
            pltpu.VMEM((rows, 4 * 8, channels), F32),
            pltpu.VMEM((3, rows, cols, channels), F32),
            pltpu.VMEM((64, channels), F32),
            pltpu.VMEM((64, channels), F32),
            pltpu.VMEM((16, channels), F32),
            pltpu.VMEM((16, channels), F32),
        ],
        compiler_params=pltpu.CompilerParams(vmem_limit_bytes=40 * 2**20),
        name="norm_conv",
    )


def make_local(count):
    def local(latent, gain, shift, weight, bias):
        rows, cols, channels = latent.shape
        out_channels = weight.shape[3]
        stride_blocks = STRIDE // cols
        tiles = -(-(count + (OVER // 2) // cols) // stride_blocks)
        tile_rows = -(-tiles // 8) * 8
        x = latent.reshape(rows * cols, channels)
        stats, edge_a, edge_b, x_near = make_stats(rows, cols, channels, tile_rows)(x)
        pairs_a = [(i, i ^ 1) for i in range(count)]
        pairs_b = []
        for i in range(1, count - 1, 2):
            pairs_b += [(i, i + 1), (i + 1, i)]
        halo_a = lax.ppermute(edge_a, "wide", pairs_a)

        def summed(stats, step):
            mask = step + 1 if 1 < step < 8 else step
            return stats + lax.ppermute(stats, "wide", [(i, i ^ mask) for i in range(count)])

        spare = jnp.zeros((-channels % 128,), F32)
        vectors = jnp.concatenate([gain, spare, shift, spare, bias, spare])
        taps = None
        step = 1
        while step < count:
            stats = summed(stats, step)
            if step == 2:
                blend, halo_a, stats = lax.optimization_barrier((blend, halo_a, stats))
            if step == 1:
                edge_b, stats = lax.optimization_barrier((edge_b, stats))
                halo_b = lax.ppermute(edge_b, "wide", pairs_b)
                blend = make_blend(cols, channels, count)(stats)
            step *= 2
            if step == 4 or (taps is None and step >= count):
                taps = make_weights(channels, out_channels)(stats, weight)
            if step == 8:
                taps, stats = lax.optimization_barrier((taps, stats))
        out = make_main(rows, cols, channels, out_channels, tile_rows, count)(
            x_near, halo_a, halo_b, stats, vectors, blend, taps
        )
        return out.reshape(rows, cols, out_channels)

    return local


def solution(mesh):
    in_specs = (P("img", "wide", None), P(), P(), P(), P())
    out_specs = P("img", "wide", None)
    return jax.shard_map(
        make_local(mesh.shape["wide"]),
        mesh=mesh,
        in_specs=in_specs,
        out_specs=out_specs,
        check_vma=False,
    )
```

```python
import jax
import jax.numpy as jnp
from jax import lax
from jax.experimental import pallas as pl
from jax.experimental.pallas import tpu as pltpu
from jax.sharding import PartitionSpec as P

NORM_GROUPS = 32
TILE = 128
OVER = 32
DIL = 8
STRIDE = 96
EPS = 1e-05
F32 = jnp.float32
BF16 = jnp.bfloat16


def iota(shape, dim):
    return lax.broadcasted_iota(jnp.int32, shape, dim)


def group_onehot(channels, per_group, offset):
    lane = iota((128, channels), 0) - offset
    first = lane * per_group
    ch = iota((128, channels), 1)
    return ((ch >= first) & (ch < first + per_group) & (lane >= 0)).astype(BF16)


def group_onehot_t(channels, per_group, offset):
    lane = iota((channels, 128), 1) - offset
    first = lane * per_group
    ch = iota((channels, 128), 0)
    return ((ch >= first) & (ch < first + per_group) & (lane >= 0)).astype(BF16)


def spread(values, onehot):
    high = values.astype(BF16)
    left = values - high.astype(F32)
    middle = left.astype(BF16)
    low = (left - middle.astype(F32)).astype(BF16)
    count = values.shape[0]
    out = jnp.dot(
        jnp.concatenate([high, middle, low], axis=0), onehot, preferred_element_type=F32
    )
    return out[:count] + out[count : 2 * count] + out[2 * count :]


def make_stats(rows, cols, channels, tile_rows):
    per_group = channels // NORM_GROUPS
    rim_blocks = (OVER // 2) // cols
    stride_blocks = STRIDE // cols
    tile_blocks = TILE // cols

    def kernel(x_ref, stats_ref, ea_ref, eb_ref, near_ref, s_ref, q_ref):
        block = lax.axis_index("wide")
        even = lax.rem(block, 2) == 0
        for a in range(0, DIL, 2):
            s = [jnp.zeros((8, channels), F32) for _ in range(2)]
            q = [jnp.zeros((8, channels), F32) for _ in range(2)]
            for rr in range(rows // DIL):
                pa, pb = [], []
                for u in range(2):
                    r = rr * DIL + a + u
                    x = x_ref[r * cols : (r + 1) * cols, :]
                    near_ref[r * cols : (r + 1) * cols, :] = x
                    x = x.astype(F32)
                    lo, hi = x[:8], x[8:]
                    s[u] += lo + hi
                    q[u] += lo * lo + hi * hi
                    pa.append(jnp.where(even, hi, lo))
                    pb.append(jnp.where(even, lo, hi))
                r0 = (rr * DIL + a) * 8
                ea_ref[r0 : r0 + 16, :] = jnp.concatenate(pa, axis=0).astype(BF16)
                eb_ref[r0 : r0 + 16, :] = jnp.concatenate(pb, axis=0).astype(BF16)
            for u in range(2):
                s_ref[(a + u) * 8 : (a + u) * 8 + 8, :] = s[u]
                q_ref[(a + u) * 8 : (a + u) * 8 + 8, :] = q[u]
        total = None
        for ref, half, offset in (
            (s_ref, 0, 0),
            (s_ref, 1, 32),
            (q_ref, 0, 64),
            (q_ref, 1, 96),
        ):
            term = spread(
                ref[half * 32 : half * 32 + 32, :],
                group_onehot_t(channels, per_group, offset),
            )
            total = term if total is None else total + term
        stats_ref[0:32, :] = total
        line = jnp.sum(total, axis=0, keepdims=True)
        line = jnp.broadcast_to(line, (8, 128))
        line = line + pltpu.roll(line, 96, 1)
        for k in range(tile_rows // 8):
            start = (iota((8, 128), 0) + 8 * k) * stride_blocks - rim_blocks
            covers = (block >= start) & (block < start + tile_blocks)
            stats_ref[32 + 8 * k : 40 + 8 * k, :] = jnp.where(covers, line, 0.0)

    return pl.pallas_call(
        kernel,
        out_shape=(
            jax.ShapeDtypeStruct((32 + tile_rows, 128), F32),
            jax.ShapeDtypeStruct((rows * 8, channels), BF16),
            jax.ShapeDtypeStruct((rows * 8, channels), BF16),
            jax.ShapeDtypeStruct((rows * cols, channels), BF16),
        ),
        scratch_shapes=[
            pltpu.VMEM((64, channels), F32),
            pltpu.VMEM((64, channels), F32),
        ],
        compiler_params=pltpu.CompilerParams(vmem_limit_bytes=16 * 2**20),
        name="block_stats",
    )


def make_blend(cols, channels, count):
    rim = OVER // 2

    def kernel(after_ref, bw_ref):
        block = lax.axis_index("wide")
        tile0 = lax.div(block + rim // cols, STRIDE // cols)
        tile1 = tile0 - 1
        sub_id = iota((8, channels), 0)
        for k in range(3):
            if k < 2:
                col = sub_id + 8 * k
            else:
                col = jnp.where(sub_id < 4, sub_id + cols, sub_id - 8)
            col = col + block * cols
            in_image = (col >= 0) & (col < count * cols)
            for j in range(3):
                out_col = col - (j - 1)
                ramps = []
                for tid in (tile0, tile1):
                    q = out_col - (tid * STRIDE - rim)
                    ok = (q >= 0) & (q < TILE) & (tid >= 0)
                    ramp = jnp.minimum(q + 1, TILE - q).astype(F32)
                    ramps.append(jnp.where(ok, ramp, 0.0))
                whole = jnp.maximum(ramps[0] + ramps[1], 1.0)
                for t, tid in enumerate((tile0, tile1)):
                    q = col - (tid * STRIDE - rim)
                    ok = (q >= 0) & (q < TILE) & in_image
                    bw_ref[j, k, t] = jnp.where(ok, ramps[t] / whole, 0.0)


    return pl.pallas_call(
        kernel,
        in_specs=[pl.BlockSpec(memory_space=pl.ANY)],
        out_specs=pl.BlockSpec(memory_space=pltpu.VMEM),
        out_shape=jax.ShapeDtypeStruct((3, 3, 2, 8, channels), F32),
        compiler_params=pltpu.CompilerParams(vmem_limit_bytes=16 * 2**20),
        cost_estimate=pl.CostEstimate(flops=5000000000, bytes_accessed=0, transcendentals=0),
        name="blend_weights",
    )


def make_weights(channels, out_channels):
    main = (channels // 128) * 128
    rem = channels - main

    def kernel(after_ref, w_hbm, w_ref, sem):
        copies = []
        for tap in range(9):
            i, j = tap // 3, tap % 3
            copies.append(
                pltpu.make_async_copy(
                    w_hbm.at[i, j, pl.ds(0, main), :],
                    w_ref.at[pl.ds(tap * main, main), :],
                    sem.at[2 * tap],
                )
            )
            copies.append(
                pltpu.make_async_copy(
                    w_hbm.at[i, j, pl.ds(main, rem), :],
                    w_ref.at[pl.ds(9 * main + tap * rem, rem), :],
                    sem.at[2 * tap + 1],
                )
            )
        for c in copies:
            c.start()

        for c in copies:
            c.wait()

    return pl.pallas_call(
        kernel,
        in_specs=[pl.BlockSpec(memory_space=pl.ANY), pl.BlockSpec(memory_space=pltpu.HBM)],
        out_specs=pl.BlockSpec(memory_space=pltpu.VMEM),
        out_shape=jax.ShapeDtypeStruct((9 * channels, out_channels), BF16),
        scratch_shapes=[pltpu.SemaphoreType.DMA((18,))],
        compiler_params=pltpu.CompilerParams(vmem_limit_bytes=50 * 2**20),
        cost_estimate=pl.CostEstimate(flops=5 * 10**9, bytes_accessed=0, transcendentals=0),
        name="conv_weights",
    )


def make_main(rows, cols, channels, out_channels, tile_rows, count):
    per_group = channels // NORM_GROUPS
    rim = OVER // 2
    rim_blocks = rim // cols
    stride_blocks = STRIDE // cols
    tile_blocks = TILE // cols
    pixels = rows * cols
    main = (channels // 128) * 128
    rem = channels - main
    depth = 9 * channels
    sub_items = float((rows // DIL) * (cols // DIL) * count * per_group)
    all_rows = 32 + tile_rows

    def kernel(
        x_ref, ha_ref, hb_ref, stats_ref, vec_ref, bw_ref, w_ref, o_ref,
        a_ref, sub_ref, blend_ref, sc_ref, sh_ref, tsc_ref, tsh_ref,
    ):
        block = lax.axis_index("wide")
        even = lax.rem(block, 2) == 0
        tile0 = lax.div(block + rim_blocks, stride_blocks)
        tile1 = tile0 - 1

        stats = stats_ref[...]
        row_id = iota((all_rows, 128), 0)
        lane_id = iota((all_rows, 128), 1)
        start = (row_id - 32) * stride_blocks - rim_blocks
        blocks = jnp.minimum(start + tile_blocks, count) - jnp.maximum(start, 0)
        tile_items = jnp.maximum(blocks, 1).astype(F32) * float(pixels * per_group)
        is_sub = row_id < 32
        items = jnp.where(is_sub, sub_items, tile_items)
        mean = stats / items
        square = pltpu.roll(stats, 64, 1) / items
        inverse = lax.rsqrt(square - mean * mean + EPS)
        valid = lane_id < jnp.where(is_sub, 64, 32)
        mean = jnp.where(valid, mean, 0.0)
        inverse = jnp.where(valid, inverse, 0.0)
        both = jnp.concatenate([mean, inverse], axis=0)
        vec = vec_ref[...].reshape(1, -1)
        wide_c = vec.shape[1] // 3
        gain = 0.5 * vec[:, :channels]
        shift = 0.5 * vec[:, wide_c : wide_c + channels]
        bias = vec[:, 2 * wide_c : 2 * wide_c + channels]
        for half in range(2):
            wide = spread(both, group_onehot(channels, per_group, 32 * half))
            scale = wide[all_rows:] * gain
            offset = shift - wide[:all_rows] * scale
            sc_ref[32 * half : 32 * half + 32, :] = scale[:32]
            sh_ref[32 * half : 32 * half + 32, :] = offset[:32]
            if half == 0:
                tile_row = iota((tile_rows, channels), 0)
                for t, tid in enumerate((tile0, tile1)):
                    pick = tile_row == jnp.maximum(tid, 0)
                    for ref, values in ((tsc_ref, scale), (tsh_ref, offset)):
                        line = jnp.sum(
                            jnp.where(pick, values[32:], 0.0), axis=0, keepdims=True
                        )
                        ref[8 * t : 8 * t + 8, :] = jnp.broadcast_to(line, (8, channels))

        left_ok = jnp.where(block > 0, 1.0, 0.0).astype(F32)
        right_ok = jnp.where(block < count - 1, 1.0, 0.0).astype(F32)

        sub_id = iota((8, channels), 0)
        def silu(x, scale, offset):
            h = x * scale + offset
            return h + h * jnp.tanh(h)

        def activate(m, tiles):
            ha = ha_ref[pl.ds(pl.multiple_of(16 * m, 16), 16), :].astype(F32)
            hb = hb_ref[pl.ds(pl.multiple_of(16 * m, 16), 16), :].astype(F32)
            left = jnp.where(even, hb, ha)
            right = jnp.where(even, ha, hb)
            for u in range(2):
                r = 2 * m + u
                x = x_ref[pl.ds(pl.multiple_of(r * cols, cols), cols), :].astype(F32)
                xl, xr = left[8 * u : 8 * u + 8], right[8 * u : 8 * u + 8]
                x0, x1 = x[:8], x[8:]
                res = pl.multiple_of(lax.rem(r, DIL) * 8, 8)
                scale = sc_ref[pl.ds(res, 8), :]
                offset = sh_ref[pl.ds(res, 8), :]
                sub_ref[r, 0:8, :] = silu(xl, scale, offset) * left_ok
                sub_ref[r, 8:16, :] = silu(x0, scale, offset)
                sub_ref[r, 16:24, :] = silu(x1, scale, offset)
                sub_ref[r, 24:32, :] = silu(xr, scale, offset) * right_ok
                xh = jnp.where(sub_id < 4, xr, xl)
                acts = [
                    [
                        silu(v, tsc_ref[8 * t : 8 * t + 8, :], tsh_ref[8 * t : 8 * t + 8, :])
                        for t in range(tiles)
                    ]
                    for v in (x0, x1, xh)
                ]

                def mix(j, k):
                    if tiles == 1:
                        return acts[k][0] if k < 2 else acts[k][0] * rim_ok
                    return bw_ref[j, k, 0] * acts[k][0] + bw_ref[j, k, 1] * acts[k][1]

                blend_ref[1, r, 0:8, :] = mix(1, 0)
                blend_ref[1, r, 8:16, :] = mix(1, 1)
                f = [pltpu.roll(mix(2, k), 7, 0) for k in range(3)]
                blend_ref[2, r, 0:8, :] = jnp.where(sub_id < 7, f[0], f[1])
                blend_ref[2, r, 8:16, :] = jnp.where(sub_id < 7, f[1], f[2])
                g = [pltpu.roll(mix(0, k), 1, 0) for k in range(3)]
                blend_ref[0, r, 0:8, :] = jnp.where(sub_id > 0, g[0], g[2])
                blend_ref[0, r, 8:16, :] = jnp.where(sub_id > 0, g[1], g[0])

        rim_col = jnp.where(sub_id < 4, sub_id + cols, sub_id - 8) + block * cols
        rim_at = rim_col - (tile0 * STRIDE - rim)
        rim_in = (rim_at >= 0) & (rim_at < TILE) & (rim_col >= 0) & (rim_col < count * cols)
        rim_ok = jnp.where(rim_in, 1.0, 0.0).astype(F32)
        shared = (tile1 >= 0) & (block < tile1 * stride_blocks - rim_blocks + tile_blocks)

        @pl.when(shared)
        def _():
            @pl.loop(0, rows // 2, unroll=2)
            def _(m):
                activate(m, 2)

        @pl.when(jnp.logical_not(shared))
        def _():
            @pl.loop(0, rows // 2, unroll=2)
            def _(m):
                activate(m, 1)

        def gather(r):
            at = pl.ds(r * cols, cols)
            held = None
            for tap in range(9):
                i, j = tap // 3, tap % 3
                near, far = r + i - 1, r + DIL * (i - 1)
                v = None
                if 0 <= near < rows:
                    v = blend_ref[j, near]
                if 0 <= far < rows:
                    w = sub_ref[far, 8 * j : 8 * j + cols, :]
                    v = w if v is None else v + w
                if v is None:
                    v = jnp.zeros((cols, channels), F32)
                v = v.astype(BF16)
                a_ref[at, tap * main : (tap + 1) * main] = v[:, :main]
                if rem:
                    base = 9 * main + tap * rem
                    if tap % 2 == 0 and tap < 8:
                        held = v[:, main:]
                    elif tap < 8:
                        a_ref[at, base - rem : base + rem] = jnp.concatenate(
                            [held, v[:, main:]], axis=1
                        )
                    else:
                        a_ref[at, base : base + rem] = v[:, main:]

        for m in range(0, rows, 8):
            for r in range(m, m + 8):
                gather(r)
            at = pl.ds(m * cols, 8 * cols)
            acc = jnp.dot(a_ref[at, :], w_ref[...], preferred_element_type=F32)
            o_ref[at, :] = (0.5 * acc + bias).astype(BF16)

    vmem = pl.BlockSpec(memory_space=pltpu.VMEM)
    return pl.pallas_call(
        kernel,
        in_specs=[vmem] * 7,
        out_specs=vmem,
        out_shape=jax.ShapeDtypeStruct((pixels, out_channels), BF16),
        scratch_shapes=[
            pltpu.VMEM((pixels, depth), BF16),
            pltpu.VMEM((rows, 4 * 8, channels), F32),
            pltpu.VMEM((3, rows, cols, channels), F32),
            pltpu.VMEM((64, channels), F32),
            pltpu.VMEM((64, channels), F32),
            pltpu.VMEM((16, channels), F32),
            pltpu.VMEM((16, channels), F32),
        ],
        compiler_params=pltpu.CompilerParams(vmem_limit_bytes=40 * 2**20),
        name="norm_conv",
    )


def make_local(count):
    def local(latent, gain, shift, weight, bias):
        rows, cols, channels = latent.shape
        out_channels = weight.shape[3]
        stride_blocks = STRIDE // cols
        tiles = -(-(count + (OVER // 2) // cols) // stride_blocks)
        tile_rows = -(-tiles // 8) * 8
        x = latent.reshape(rows * cols, channels)
        stats, edge_a, edge_b, x_near = make_stats(rows, cols, channels, tile_rows)(x)
        pairs_a = [(i, i ^ 1) for i in range(count)]
        pairs_b = []
        for i in range(1, count - 1, 2):
            pairs_b += [(i, i + 1), (i + 1, i)]
        halo_a = lax.ppermute(edge_a, "wide", pairs_a)

        def summed(stats, step):
            mask = step + 1 if 1 < step < 8 else step
            return stats + lax.ppermute(stats, "wide", [(i, i ^ mask) for i in range(count)])

        spare = jnp.zeros((-channels % 128,), F32)
        vectors = jnp.concatenate([gain, spare, shift, spare, bias, spare])
        taps = None
        step = 1
        while step < count:
            stats = summed(stats, step)
            if step == 2:
                blend, halo_a, stats = lax.optimization_barrier((blend, halo_a, stats))
            if step == 1:
                edge_b, stats = lax.optimization_barrier((edge_b, stats))
                halo_b = lax.ppermute(edge_b, "wide", pairs_b)
                blend = make_blend(cols, channels, count)(stats)
            step *= 2
            if step == 4 or (taps is None and step >= count):
                taps = make_weights(channels, out_channels)(stats, weight)
            if step == 8:
                taps, stats = lax.optimization_barrier((taps, stats))
        out = make_main(rows, cols, channels, out_channels, tile_rows, count)(
            x_near, halo_a, halo_b, stats, vectors, blend, taps
        )
        return out.reshape(rows, cols, out_channels)

    return local


def solution(mesh):
    in_specs = (P("img", "wide", None), P(), P(), P(), P())
    out_specs = P("img", "wide", None)
    return jax.shard_map(
        make_local(mesh.shape["wide"]),
        mesh=mesh,
        in_specs=in_specs,
        out_specs=out_specs,
        check_vma=False,
    )
```

```python
import jax
import jax.numpy as jnp
from jax import lax
from jax.experimental import pallas as pl
from jax.experimental.pallas import tpu as pltpu
from jax.sharding import PartitionSpec as P

NORM_GROUPS = 32
TILE = 128
OVER = 32
DIL = 8
STRIDE = 96
EPS = 1e-05
F32 = jnp.float32
BF16 = jnp.bfloat16


def iota(shape, dim):
    return lax.broadcasted_iota(jnp.int32, shape, dim)


def group_onehot(channels, per_group, offset):
    lane = iota((128, channels), 0) - offset
    first = lane * per_group
    ch = iota((128, channels), 1)
    return ((ch >= first) & (ch < first + per_group) & (lane >= 0)).astype(BF16)


def group_onehot_t(channels, per_group, offset):
    lane = iota((channels, 128), 1) - offset
    first = lane * per_group
    ch = iota((channels, 128), 0)
    return ((ch >= first) & (ch < first + per_group) & (lane >= 0)).astype(BF16)


def spread(values, onehot):
    high = values.astype(BF16)
    left = values - high.astype(F32)
    middle = left.astype(BF16)
    low = (left - middle.astype(F32)).astype(BF16)
    count = values.shape[0]
    out = jnp.dot(
        jnp.concatenate([high, middle, low], axis=0), onehot, preferred_element_type=F32
    )
    return out[:count] + out[count : 2 * count] + out[2 * count :]


def make_stats(rows, cols, channels, tile_rows):
    per_group = channels // NORM_GROUPS
    rim_blocks = (OVER // 2) // cols
    stride_blocks = STRIDE // cols
    tile_blocks = TILE // cols

    def kernel(x_ref, stats_ref, ea_ref, eb_ref, near_ref, s_ref, q_ref):
        block = lax.axis_index("wide")
        even = lax.rem(block, 2) == 0
        for a in range(0, DIL, 2):
            s = [jnp.zeros((8, channels), F32) for _ in range(2)]
            q = [jnp.zeros((8, channels), F32) for _ in range(2)]
            for rr in range(rows // DIL):
                pa, pb = [], []
                for u in range(2):
                    r = rr * DIL + a + u
                    x = x_ref[r * cols : (r + 1) * cols, :]
                    near_ref[r * cols : (r + 1) * cols, :] = x
                    x = x.astype(F32)
                    lo, hi = x[:8], x[8:]
                    s[u] += lo + hi
                    q[u] += lo * lo + hi * hi
                    pa.append(jnp.where(even, hi, lo))
                    pb.append(jnp.where(even, lo, hi))
                r0 = (rr * DIL + a) * 8
                ea_ref[r0 : r0 + 16, :] = jnp.concatenate(pa, axis=0).astype(BF16)
                eb_ref[r0 : r0 + 16, :] = jnp.concatenate(pb, axis=0).astype(BF16)
            for u in range(2):
                s_ref[(a + u) * 8 : (a + u) * 8 + 8, :] = s[u]
                q_ref[(a + u) * 8 : (a + u) * 8 + 8, :] = q[u]
        total = None
        for ref, half, offset in (
            (s_ref, 0, 0),
            (s_ref, 1, 32),
            (q_ref, 0, 64),
            (q_ref, 1, 96),
        ):
            term = spread(
                ref[half * 32 : half * 32 + 32, :],
                group_onehot_t(channels, per_group, offset),
            )
            total = term if total is None else total + term
        stats_ref[0:32, :] = total
        line = jnp.sum(total, axis=0, keepdims=True)
        line = jnp.broadcast_to(line, (8, 128))
        line = line + pltpu.roll(line, 96, 1)
        for k in range(tile_rows // 8):
            start = (iota((8, 128), 0) + 8 * k) * stride_blocks - rim_blocks
            covers = (block >= start) & (block < start + tile_blocks)
            stats_ref[32 + 8 * k : 40 + 8 * k, :] = jnp.where(covers, line, 0.0)

    return pl.pallas_call(
        kernel,
        out_shape=(
            jax.ShapeDtypeStruct((32 + tile_rows, 128), F32),
            jax.ShapeDtypeStruct((rows * 8, channels), BF16),
            jax.ShapeDtypeStruct((rows * 8, channels), BF16),
            jax.ShapeDtypeStruct((rows * cols, channels), BF16),
        ),
        scratch_shapes=[
            pltpu.VMEM((64, channels), F32),
            pltpu.VMEM((64, channels), F32),
        ],
        compiler_params=pltpu.CompilerParams(vmem_limit_bytes=16 * 2**20),
        name="block_stats",
    )


def make_blend(cols, channels, count):
    rim = OVER // 2

    def kernel(after_ref, bw_ref):
        block = lax.axis_index("wide")
        tile0 = lax.div(block + rim // cols, STRIDE // cols)
        tile1 = tile0 - 1
        sub_id = iota((8, 128), 0)
        for k in range(3):
            if k < 2:
                col = sub_id + 8 * k
            else:
                col = jnp.where(sub_id < 4, sub_id + cols, sub_id - 8)
            col = col + block * cols
            in_image = (col >= 0) & (col < count * cols)
            for j in range(3):
                out_col = col - (j - 1)
                ramps = []
                for tid in (tile0, tile1):
                    q = out_col - (tid * STRIDE - rim)
                    ok = (q >= 0) & (q < TILE) & (tid >= 0)
                    ramp = jnp.minimum(q + 1, TILE - q).astype(F32)
                    ramps.append(jnp.where(ok, ramp, 0.0))
                whole = jnp.maximum(ramps[0] + ramps[1], 1.0)
                for t, tid in enumerate((tile0, tile1)):
                    q = col - (tid * STRIDE - rim)
                    ok = (q >= 0) & (q < TILE) & in_image
                    bw_ref[j, k, t] = jnp.where(ok, ramps[t] / whole, 0.0)


    return pl.pallas_call(
        kernel,
        in_specs=[pl.BlockSpec(memory_space=pl.ANY)],
        out_specs=pl.BlockSpec(memory_space=pltpu.VMEM),
        out_shape=jax.ShapeDtypeStruct((3, 3, 2, 8, 128), F32),
        compiler_params=pltpu.CompilerParams(vmem_limit_bytes=16 * 2**20),
        cost_estimate=pl.CostEstimate(flops=5000000000, bytes_accessed=0, transcendentals=0),
        name="blend_weights",
    )


def make_weights(channels, out_channels):
    main = (channels // 128) * 128
    rem = channels - main

    def kernel(after_ref, w_hbm, w_ref, sem):
        copies = []
        for tap in range(9):
            i, j = tap // 3, tap % 3
            copies.append(
                pltpu.make_async_copy(
                    w_hbm.at[i, j, pl.ds(0, main), :],
                    w_ref.at[pl.ds(tap * main, main), :],
                    sem.at[2 * tap],
                )
            )
            copies.append(
                pltpu.make_async_copy(
                    w_hbm.at[i, j, pl.ds(main, rem), :],
                    w_ref.at[pl.ds(9 * main + tap * rem, rem), :],
                    sem.at[2 * tap + 1],
                )
            )
        for c in copies:
            c.start()

        for c in copies:
            c.wait()

    return pl.pallas_call(
        kernel,
        in_specs=[pl.BlockSpec(memory_space=pl.ANY), pl.BlockSpec(memory_space=pltpu.HBM)],
        out_specs=pl.BlockSpec(memory_space=pltpu.VMEM),
        out_shape=jax.ShapeDtypeStruct((9 * channels, out_channels), BF16),
        scratch_shapes=[pltpu.SemaphoreType.DMA((18,))],
        compiler_params=pltpu.CompilerParams(vmem_limit_bytes=50 * 2**20),
        cost_estimate=pl.CostEstimate(flops=5 * 10**9, bytes_accessed=0, transcendentals=0),
        name="conv_weights",
    )


def make_main(rows, cols, channels, out_channels, tile_rows, count):
    per_group = channels // NORM_GROUPS
    rim = OVER // 2
    rim_blocks = rim // cols
    stride_blocks = STRIDE // cols
    tile_blocks = TILE // cols
    pixels = rows * cols
    main = (channels // 128) * 128
    rem = channels - main
    depth = 9 * channels
    sub_items = float((rows // DIL) * (cols // DIL) * count * per_group)
    all_rows = 32 + tile_rows

    def kernel(
        x_ref, ha_ref, hb_ref, stats_ref, vec_ref, bw_ref, w_ref, o_ref,
        a_ref, sub_ref, blend_ref, sc_ref, sh_ref, tsc_ref, tsh_ref,
    ):
        block = lax.axis_index("wide")
        even = lax.rem(block, 2) == 0
        tile0 = lax.div(block + rim_blocks, stride_blocks)
        tile1 = tile0 - 1

        stats = stats_ref[...]
        row_id = iota((all_rows, 128), 0)
        lane_id = iota((all_rows, 128), 1)
        start = (row_id - 32) * stride_blocks - rim_blocks
        blocks = jnp.minimum(start + tile_blocks, count) - jnp.maximum(start, 0)
        tile_items = jnp.maximum(blocks, 1).astype(F32) * float(pixels * per_group)
        is_sub = row_id < 32
        items = jnp.where(is_sub, sub_items, tile_items)
        mean = stats / items
        square = pltpu.roll(stats, 64, 1) / items
        inverse = lax.rsqrt(square - mean * mean + EPS)
        valid = lane_id < jnp.where(is_sub, 64, 32)
        mean = jnp.where(valid, mean, 0.0)
        inverse = jnp.where(valid, inverse, 0.0)
        both = jnp.concatenate([mean, inverse], axis=0)
        vec = vec_ref[...].reshape(1, -1)
        wide_c = vec.shape[1] // 3
        gain = 0.5 * vec[:, :channels]
        shift = 0.5 * vec[:, wide_c : wide_c + channels]
        bias = vec[:, 2 * wide_c : 2 * wide_c + channels]
        for half in range(2):
            wide = spread(both, group_onehot(channels, per_group, 32 * half))
            scale = wide[all_rows:] * gain
            offset = shift - wide[:all_rows] * scale
            sc_ref[32 * half : 32 * half + 32, :] = scale[:32]
            sh_ref[32 * half : 32 * half + 32, :] = offset[:32]
            if half == 0:
                tile_row = iota((tile_rows, channels), 0)
                for t, tid in enumerate((tile0, tile1)):
                    pick = tile_row == jnp.maximum(tid, 0)
                    for ref, values in ((tsc_ref, scale), (tsh_ref, offset)):
                        line = jnp.sum(
                            jnp.where(pick, values[32:], 0.0), axis=0, keepdims=True
                        )
                        ref[8 * t : 8 * t + 8, :] = jnp.broadcast_to(line, (8, channels))

        left_ok = jnp.where(block > 0, 1.0, 0.0).astype(F32)
        right_ok = jnp.where(block < count - 1, 1.0, 0.0).astype(F32)

        sub_id = iota((8, channels), 0)
        def weight(j, k, t):
            w = bw_ref[j, k, t]
            parts = [w] * (channels // 128) + ([w[:, :rem]] if rem else [])
            return jnp.concatenate(parts, axis=1)

        def silu(x, scale, offset):
            h = x * scale + offset
            return h + h * jnp.tanh(h)

        def activate(m, tiles):
            ha = ha_ref[pl.ds(pl.multiple_of(16 * m, 16), 16), :].astype(F32)
            hb = hb_ref[pl.ds(pl.multiple_of(16 * m, 16), 16), :].astype(F32)
            left = jnp.where(even, hb, ha)
            right = jnp.where(even, ha, hb)
            for u in range(2):
                r = 2 * m + u
                x = x_ref[pl.ds(pl.multiple_of(r * cols, cols), cols), :].astype(F32)
                xl, xr = left[8 * u : 8 * u + 8], right[8 * u : 8 * u + 8]
                x0, x1 = x[:8], x[8:]
                res = pl.multiple_of(lax.rem(r, DIL) * 8, 8)
                scale = sc_ref[pl.ds(res, 8), :]
                offset = sh_ref[pl.ds(res, 8), :]
                sub_ref[r, 0:8, :] = silu(xl, scale, offset) * left_ok
                sub_ref[r, 8:16, :] = silu(x0, scale, offset)
                sub_ref[r, 16:24, :] = silu(x1, scale, offset)
                sub_ref[r, 24:32, :] = silu(xr, scale, offset) * right_ok
                xh = jnp.where(sub_id < 4, xr, xl)
                acts = [
                    [
                        silu(v, tsc_ref[8 * t : 8 * t + 8, :], tsh_ref[8 * t : 8 * t + 8, :])
                        for t in range(tiles)
                    ]
                    for v in (x0, x1, xh)
                ]

                def mix(j, k):
                    if tiles == 1:
                        return acts[k][0] if k < 2 else acts[k][0] * rim_ok
                    return weight(j, k, 0) * acts[k][0] + weight(j, k, 1) * acts[k][1]

                blend_ref[1, r, 0:8, :] = mix(1, 0)
                blend_ref[1, r, 8:16, :] = mix(1, 1)
                f = [pltpu.roll(mix(2, k), 7, 0) for k in range(3)]
                blend_ref[2, r, 0:8, :] = jnp.where(sub_id < 7, f[0], f[1])
                blend_ref[2, r, 8:16, :] = jnp.where(sub_id < 7, f[1], f[2])
                g = [pltpu.roll(mix(0, k), 1, 0) for k in range(3)]
                blend_ref[0, r, 0:8, :] = jnp.where(sub_id > 0, g[0], g[2])
                blend_ref[0, r, 8:16, :] = jnp.where(sub_id > 0, g[1], g[0])

        rim_col = jnp.where(sub_id < 4, sub_id + cols, sub_id - 8) + block * cols
        rim_at = rim_col - (tile0 * STRIDE - rim)
        rim_in = (rim_at >= 0) & (rim_at < TILE) & (rim_col >= 0) & (rim_col < count * cols)
        rim_ok = jnp.where(rim_in, 1.0, 0.0).astype(F32)
        shared = (tile1 >= 0) & (block < tile1 * stride_blocks - rim_blocks + tile_blocks)

        @pl.when(shared)
        def _():
            @pl.loop(0, rows // 2, unroll=2)
            def _(m):
                activate(m, 2)

        @pl.when(jnp.logical_not(shared))
        def _():
            @pl.loop(0, rows // 2, unroll=2)
            def _(m):
                activate(m, 1)

        def gather(r):
            at = pl.ds(r * cols, cols)
            held = None
            for tap in range(9):
                i, j = tap // 3, tap % 3
                near, far = r + i - 1, r + DIL * (i - 1)
                v = None
                if 0 <= near < rows:
                    v = blend_ref[j, near]
                if 0 <= far < rows:
                    w = sub_ref[far, 8 * j : 8 * j + cols, :]
                    v = w if v is None else v + w
                if v is None:
                    v = jnp.zeros((cols, channels), F32)
                v = v.astype(BF16)
                a_ref[at, tap * main : (tap + 1) * main] = v[:, :main]
                if rem:
                    base = 9 * main + tap * rem
                    if tap % 2 == 0 and tap < 8:
                        held = v[:, main:]
                    elif tap < 8:
                        a_ref[at, base - rem : base + rem] = jnp.concatenate(
                            [held, v[:, main:]], axis=1
                        )
                    else:
                        a_ref[at, base : base + rem] = v[:, main:]

        for m in range(0, rows, 8):
            for r in range(m, m + 8):
                gather(r)
            at = pl.ds(m * cols, 8 * cols)
            acc = jnp.dot(a_ref[at, :], w_ref[...], preferred_element_type=F32)
            o_ref[at, :] = (0.5 * acc + bias).astype(BF16)

    vmem = pl.BlockSpec(memory_space=pltpu.VMEM)
    return pl.pallas_call(
        kernel,
        in_specs=[vmem] * 7,
        out_specs=vmem,
        out_shape=jax.ShapeDtypeStruct((pixels, out_channels), BF16),
        scratch_shapes=[
            pltpu.VMEM((pixels, depth), BF16),
            pltpu.VMEM((rows, 4 * 8, channels), F32),
            pltpu.VMEM((3, rows, cols, channels), F32),
            pltpu.VMEM((64, channels), F32),
            pltpu.VMEM((64, channels), F32),
            pltpu.VMEM((16, channels), F32),
            pltpu.VMEM((16, channels), F32),
        ],
        compiler_params=pltpu.CompilerParams(vmem_limit_bytes=40 * 2**20),
        name="norm_conv",
    )


def make_local(count):
    def local(latent, gain, shift, weight, bias):
        rows, cols, channels = latent.shape
        out_channels = weight.shape[3]
        stride_blocks = STRIDE // cols
        tiles = -(-(count + (OVER // 2) // cols) // stride_blocks)
        tile_rows = -(-tiles // 8) * 8
        x = latent.reshape(rows * cols, channels)
        stats, edge_a, edge_b, x_near = make_stats(rows, cols, channels, tile_rows)(x)
        pairs_a = [(i, i ^ 1) for i in range(count)]
        pairs_b = []
        for i in range(1, count - 1, 2):
            pairs_b += [(i, i + 1), (i + 1, i)]
        halo_a = lax.ppermute(edge_a, "wide", pairs_a)

        def summed(stats, step):
            mask = step + 1 if 1 < step < 8 else step
            return stats + lax.ppermute(stats, "wide", [(i, i ^ mask) for i in range(count)])

        spare = jnp.zeros((-channels % 128,), F32)
        vectors = jnp.concatenate([gain, spare, shift, spare, bias, spare])
        taps = None
        step = 1
        while step < count:
            stats = summed(stats, step)
            if step == 2:
                blend, halo_a, stats = lax.optimization_barrier((blend, halo_a, stats))
            if step == 1:
                edge_b, stats = lax.optimization_barrier((edge_b, stats))
                halo_b = lax.ppermute(edge_b, "wide", pairs_b)
                blend = make_blend(cols, channels, count)(stats)
            step *= 2
            if step == 4 or (taps is None and step >= count):
                taps = make_weights(channels, out_channels)(stats, weight)
            if step == 8:
                taps, stats = lax.optimization_barrier((taps, stats))
        out = make_main(rows, cols, channels, out_channels, tile_rows, count)(
            x_near, halo_a, halo_b, stats, vectors, blend, taps
        )
        return out.reshape(rows, cols, out_channels)

    return local


def solution(mesh):
    in_specs = (P("img", "wide", None), P(), P(), P(), P())
    out_specs = P("img", "wide", None)
    return jax.shard_map(
        make_local(mesh.shape["wide"]),
        mesh=mesh,
        in_specs=in_specs,
        out_specs=out_specs,
        check_vma=False,
    )
```
